256 devices in a mesh: chan: 32 (over x, y, core), tm: 8 (over z).
Axes of the slice: x: 4, y: 4, z: 8, core: 2. Of those that a mesh axis runs over, the one named last changes fastest.
Arguments:
- visibilities: bfloat16 [384, 2, 6144, 128], P('chan', None, 'tm'), may hold values from -6 to 6
- vis_weight: bfloat16 [6144, 128], P('tm'), may hold values from 0.19921875 to 2
- tile_index: int32 [6144], P('tm'), may hold values from 0 to 255
- tile_offset: int32 [6144, 128], P('tm'), may hold values from 0 to 255
- live_count: int32 [8, 768], P('tm'), may hold values from 1 to 128, 49152 in all within a row
Outputs:
- spectra: float32 [2, 384, 65536], P(None, None, ('tm', 'chan'))
The draws below stay inside these ranges and needn't reach their ends.
Inputs may be any that keep to these rules, and one draw needn't show every extreme that they name: `live_count`: in each time span the counts sum to 49152, and some group holds all 128 slots.
All inputs are finite; a program needn't handle non-finite values.
Results may differ from the reference program's by a relative error of at most 0.0033.
Values sent between devices are 32-bit elements; how exact they have to be, the bound alone decides.
A program may use at most 64 MiB of HBM per device.

```python
import math
import jax
import jax.numpy as jnp
import numpy as np
from jax import lax

CHANNELS = 384
TSIDE = 16
TILE = 256
VT = 128
GRP_DEV = 768
GROUPS = 6144
NTILE = 256
UV = 65536
N_TM = 8


def with_ends(result, key, low, top_value):
    place = [jax.random.randint(jax.random.fold_in(key, axis), (), 0, length) for axis, length in enumerate(result.shape)]
    longest = result.shape.index(max(result.shape))
    next_to = place[:longest] + [(place[longest] + 1) % result.shape[longest]] + place[longest + 1:]
    return result.at[tuple(place)].set(low).at[tuple(next_to)].set(top_value)


def levels(key, shape, cuts, smallest, largest):
    def one(position, parts):
        heights = jax.random.uniform(jax.random.fold_in(jax.random.fold_in(key, 6), position), (parts,), jnp.float32, smallest / len(cuts), largest / len(cuts))
        return jnp.repeat(jnp.exp(heights), shape[position] // parts).reshape((-1,) + (1,) * (len(shape) - position - 1))

    level = one(*cuts[0])
    for cut in cuts[1:]:
        level = level * one(*cut)
    return level


def rank_table(amount, lean):
    portions = [(1 << 20) // math.isqrt(standing ** lean) + 1 for standing in range(1, amount + 1)]
    spread = 1 + sum(portions) // (1 << 30)
    return np.cumsum(np.array([max(1, weight // spread) for weight in portions]))


def ranked_ids(rng, dims, count, slope):
    table = rank_table(count, slope)
    pick = jax.random.randint(jax.random.fold_in(rng, 1), dims, 0, int(table[count - 1]))
    standing = jnp.searchsorted(jnp.asarray(table, jnp.int32), pick, side="right")
    return jax.random.permutation(jax.random.fold_in(rng, 2), count)[standing].astype(jnp.int32)


def length_profile(amount, total, most, skew):
    portions = [(1 << 20) // math.isqrt(standing ** skew) + 1 for standing in range(2, amount + 1)]
    spare, given = total - most - (amount - 1), [1] * (amount - 1)
    while spare > 0:
        candidates = [i for i in range(amount - 1) if given[i] < most]
        mass, remaining = sum([portions[i] for i in candidates]), spare
        for i in candidates:
            more = min(most - given[i], max(1, remaining * portions[i] // mass), spare)
            given[i] = given[i] + more
            spare = spare - more
    return np.array([most] + given)


def ragged(stream_key, amount, total, most, slope):
    if amount == 2:
        one = jax.random.randint(stream_key, (), max(1, total - most), min(most, total - 1) + 1)
        return jnp.stack([one, total - one])
    sizes = jnp.asarray(length_profile(amount, total, most, slope), jnp.int32)
    pairs = (amount - 1) // 2
    source_of, sink = sizes[1:1 + 2 * pairs:2], sizes[2:2 + 2 * pairs:2]
    room = jnp.minimum(source_of - 1, most - sink)
    passed = jax.random.randint(jax.random.fold_in(stream_key, 1), (pairs,), 0, 1 << 20) % (room + 1)
    sizes = sizes.at[1:1 + 2 * pairs:2].set(source_of - passed).at[2:2 + 2 * pairs:2].set(sink + passed)
    return sizes[jax.random.permutation(jax.random.fold_in(stream_key, 2), amount)]


def bell_draw(rng, extent, width, limit, shards=(), held_as=jnp.bfloat16):
    result = width * jax.random.normal(rng, extent, jnp.float32)
    if shards:
        result = result * levels(rng, extent, shards, -0.22, 0.18)
    return jnp.clip(result, -limit, limit).astype(held_as)


def setup_inputs(seed: int = 0) -> dict:
    arg_keys = jax.random.split(jax.random.key(seed), 6)
    return {
        "visibilities": bell_draw(arg_keys[0], (CHANNELS, 2, GROUPS, VT), 1.0, 6.0, ((0, 32), (2, 8))),
        "vis_weight": jnp.clip(jnp.exp(math.log(2.0) - 2.306499 * jax.random.uniform(arg_keys[1], (GROUPS, VT), jnp.float32) ** levels(arg_keys[1], (GROUPS, VT), ((0, 8),), -0.2, 0.2)), 0.19921875, 2.0).astype(jnp.bfloat16),
        "tile_index": with_ends(ranked_ids(arg_keys[2], (GROUPS,), NTILE, 2), jax.random.fold_in(arg_keys[2], 3), 0, NTILE - 1).astype(jnp.int32),
        "tile_offset": with_ends(jax.random.randint(arg_keys[3], (GROUPS, VT), 0, TILE), jax.random.fold_in(arg_keys[3], 1), 0, TILE - 1).astype(jnp.int32),
        "live_count": jax.vmap(lambda own: ragged(own, GRP_DEV, GRP_DEV * VT // 2, VT, 2))(jax.random.split(arg_keys[4], N_TM)).reshape((N_TM, GRP_DEV)).astype(jnp.int32),
    }


kernel_sigma2 = 1.44
kernel_reach = 3.0


def kernel_tile(offsets, weights, counts, side, slots):
    cells = jnp.arange(side * side, dtype=jnp.int32)
    cell_u = (cells // side).astype(jnp.float32)
    cell_v = (cells % side).astype(jnp.float32)
    cent_u = (offsets // side).astype(jnp.float32)
    cent_v = (offsets % side).astype(jnp.float32)
    delta_u = cell_u[None, None, :] - cent_u[:, :, None]
    delta_v = cell_v[None, None, :] - cent_v[:, :, None]
    inside = (jnp.abs(delta_u) <= kernel_reach) & (jnp.abs(delta_v) <= kernel_reach)
    live = jnp.arange(slots, dtype=jnp.int32)[None, :] < counts[:, None]
    shape = jnp.exp(-(delta_u * delta_u + delta_v * delta_v) / (2.0 * kernel_sigma2))
    value = weights.astype(jnp.float32)[:, :, None] * shape
    return jnp.where(inside & live[:, :, None], value, 0.0).astype(jnp.bfloat16)


def reference(visibilities, vis_weight, tile_index, tile_offset, live_count):
    rows = 2 * CHANNELS
    data = visibilities.reshape(rows, GROUPS, VT)
    counts = live_count.reshape(GROUPS)
    block = math.gcd(GROUPS, 32)

    def step(index, carry):
        grid, weight_grid = carry
        start = index * block
        piece = lax.dynamic_slice_in_dim(data, start, block, 1).astype(jnp.float32)
        kernel = kernel_tile(lax.dynamic_slice_in_dim(tile_offset, start, block, 0),
                             lax.dynamic_slice_in_dim(vis_weight, start, block, 0),
                             lax.dynamic_slice_in_dim(counts, start, block, 0), TSIDE, VT)
        kernel32 = kernel.astype(jnp.float32)
        tile_sum = jnp.einsum('rgv,gvc->grc', piece, kernel32)
        tiles = lax.dynamic_slice_in_dim(tile_index, start, block, 0)
        grid = grid.at[tiles].add(tile_sum)
        weight_grid = weight_grid.at[tiles].add(jnp.sum(kernel32, axis=1))
        return grid, weight_grid

    grid = jnp.zeros((NTILE, rows, TILE), jnp.float32)
    weight_grid = jnp.zeros((NTILE, TILE), jnp.float32)
    grid, weight_grid = lax.fori_loop(0, GROUPS // block, step, (grid, weight_grid))
    normalized = grid / jnp.maximum(weight_grid, 1.0)[:, None, :]
    shaped = normalized.reshape(NTILE, CHANNELS, 2, TILE)
    freq = jnp.arange(CHANNELS, dtype=jnp.float32)
    phase = 2.0 * jnp.pi * freq / (CHANNELS - 1)
    taper = 0.42323 - 0.49755 * jnp.cos(phase) + 0.07922 * jnp.cos(2.0 * phase)
    signal = (shaped[:, :, 0, :] + 1j * shaped[:, :, 1, :]) * taper[None, :, None]
    transform = jnp.fft.fft(signal, axis=1)
    real_part = jnp.transpose(jnp.real(transform), (1, 0, 2)).reshape(CHANNELS, UV)
    imag_part = jnp.transpose(jnp.imag(transform), (1, 0, 2)).reshape(CHANNELS, UV)
    return jnp.stack([real_part, imag_part], axis=0).astype(jnp.float32)
```

```python
import functools
import math

import jax
import jax.numpy as jnp
import ml_dtypes
import numpy as np
from jax import lax
from jax.experimental import pallas as pl
from jax.experimental.pallas import tpu as pltpu
from jax.sharding import PartitionSpec as P

TSIDE = 16
TILE = TSIDE * TSIDE
LANES = 128
KERNEL_SIGMA2 = 1.44
KERNEL_REACH = 3
HALVES = 2
MESH = pl.DeviceIdType.MESH


def split_bf16(table):
    high = table.astype(ml_dtypes.bfloat16)
    low = (table - high.astype(np.float64)).astype(ml_dtypes.bfloat16)
    return np.stack([high, low])


def spread_table():
    step = np.arange(TSIDE)[:, None] - np.arange(TSIDE)[None, :]
    line = np.where(np.abs(step) <= KERNEL_REACH, np.exp(-step * step / (2.0 * KERNEL_SIGMA2)), 0.0)
    return np.kron(line, line)


def delay_table(channels):
    freq = np.arange(channels)
    angle = 2.0 * np.pi * (freq[:, None] * freq[None, :] % channels) / channels
    phase = 2.0 * np.pi * freq / (channels - 1)
    taper = 0.42323 - 0.49755 * np.cos(phase) + 0.07922 * np.cos(2.0 * phase)
    cos_part = np.cos(angle) * taper[None, :]
    sin_part = np.sin(angle) * taper[None, :]
    upper = np.stack([cos_part, sin_part], axis=-1)
    lower = np.stack([-sin_part, cos_part], axis=-1)
    return np.stack([upper, lower], axis=0).reshape(2 * channels, 2 * channels)


def grid_kernel(tile_ref, live_ref, vis_ref, weight_ref, offset_ref, grid_ref, wgrid_ref):
    step = pl.program_id(0)
    rows, block = vis_ref.shape[0], vis_ref.shape[1]

    @pl.when(step == 0)
    def _():
        grid_ref[...] = jnp.zeros_like(grid_ref)
        wgrid_ref[...] = jnp.zeros_like(wgrid_ref)

    cell = lax.broadcasted_iota(jnp.int32, (LANES, LANES), 0).astype(jnp.int16)
    lane = lax.broadcasted_iota(jnp.int32, (8, LANES), 1)
    half = lax.broadcasted_iota(jnp.int32, (8, LANES), 0)
    zero = jnp.zeros((16, LANES), jnp.bfloat16)

    def some(index, _):
        first = pl.multiple_of(index * 16, 16)
        data = jnp.swapaxes(vis_ref[:, pl.ds(first, 16), :].astype(jnp.float32), 0, 1)
        weights = weight_ref[pl.ds(first, 16), :].astype(jnp.float32)
        for j in range(16):
            group = step * block + first + j
            weight = jnp.where(lane < live_ref[group], jnp.broadcast_to(weights[j:j + 1], (8, LANES)), 0.0)
            offset = jnp.broadcast_to(offset_ref[pl.ds(first + j, 1), :], (8, LANES))
            low = jnp.bitwise_and(offset, LANES - 1)
            high = jnp.right_shift(offset, 7)
            low16 = jnp.concatenate([low, low], 0).astype(jnp.int16)
            weight16 = jnp.concatenate([weight, weight], 0).astype(jnp.bfloat16)
            hot = jnp.concatenate(
                [jnp.where(cell[16 * k:16 * k + 16] == low16, weight16, zero) for k in range(8)], 0
            )
            parts = [
                jnp.where(high == a, data[j, 8 * q:8 * q + 8], 0.0)
                for a in range(HALVES)
                for q in range(rows // 8)
            ]
            parts.append(jnp.where(high == half, 1.0, 0.0))
            left = jnp.concatenate(parts, 0).astype(jnp.bfloat16)
            total = lax.dot_general(left, hot, (((1,), (1,)), ((), ())), preferred_element_type=jnp.float32)
            tile = tile_ref[group]
            grid_ref[tile] += total[:HALVES * rows]
            wgrid_ref[tile] += total[HALVES * rows:]
        return 0

    lax.fori_loop(0, block // 16, some, 0, unroll=True)


def gridding(data, weight, tiles, offset, live, n_tile):
    rows, groups, slots = data.shape
    block = math.gcd(groups, 64)
    return pl.pallas_call(
        grid_kernel,
        grid_spec=pltpu.PrefetchScalarGridSpec(
            num_scalar_prefetch=2,
            grid=(groups // block,),
            in_specs=[
                pl.BlockSpec((rows, block, slots), lambda i, *_: (0, i, 0)),
                pl.BlockSpec((block, slots), lambda i, *_: (i, 0)),
                pl.BlockSpec((block, slots), lambda i, *_: (i, 0)),
            ],
            out_specs=[
                pl.BlockSpec((n_tile, HALVES * rows, LANES), lambda i, *_: (0, 0, 0), pipeline_mode=pl.Buffered(1)),
                pl.BlockSpec((n_tile, 8, LANES), lambda i, *_: (0, 0, 0), pipeline_mode=pl.Buffered(1)),
            ],
        ),
        out_shape=[
            jax.ShapeDtypeStruct((n_tile, HALVES * rows, LANES), jnp.float32),
            jax.ShapeDtypeStruct((n_tile, 8, LANES), jnp.float32),
        ],
        compiler_params=pltpu.CompilerParams(vmem_limit_bytes=20 << 20),
        cost_estimate=pl.CostEstimate(flops=2 * groups * rows * slots * TILE, bytes_accessed=data.size * 2, transcendentals=0),
        name="gridding",
    )(tiles, live, data, weight, offset)


def dot3(left, right):
    dot = functools.partial(jnp.dot, preferred_element_type=jnp.float32)
    return dot(left[0], right[0]) + (dot(left[0], right[1]) + dot(left[1], right[0]))


def pair(x):
    high = x.astype(jnp.bfloat16)
    return high, (x - high.astype(jnp.float32)).astype(jnp.bfloat16)


def exchange_kernel(
    n_time, n_chan, per, grid_ref, wgrid_ref, delay_hbm, spread_hbm, out_ref,
    ring, mine, gathered, wparts, delay, spread,
    ring_send, ring_recv, plane_send, plane_recv, w_send, w_recv, table_sem,
):
    me_t = lax.axis_index("tm")
    me_c = lax.axis_index("chan")
    pieces = n_chan // per
    reach = n_time // 2
    rows2 = grid_ref.shape[1]
    rows = rows2 // HALVES
    turn = me_c // per
    neighbour = (lax.rem(me_t + 1, n_time), lax.rem(me_t + n_time - 1, n_time))

    tables = [pltpu.make_async_copy(delay_hbm, delay, table_sem.at[0]),
              pltpu.make_async_copy(spread_hbm, spread, table_sem.at[1])]
    for copy in tables:
        copy.start()

    barrier = pltpu.get_barrier_semaphore()

    def greet_t(k, _):
        pl.semaphore_signal(barrier, inc=1, device_id={"tm": lax.rem(me_t + k, n_time)}, device_id_type=MESH)
        return 0

    def greet_c(k, _):
        pl.semaphore_signal(barrier, inc=1, device_id={"chan": lax.rem(me_c + k, n_chan)}, device_id_type=MESH)
        return 0

    lax.fori_loop(1, n_time, greet_t, 0)
    lax.fori_loop(1, n_chan, greet_c, 0)
    pl.semaphore_wait(barrier, n_time - 1 + n_chan - 1)

    def span(slot):
        return pl.ds(lax.rem(slot + turn, pieces) * per, per)

    def grid_span(chunk, slot):
        return pl.ds(chunk * n_chan + lax.rem(slot + turn, pieces) * per, per)

    def chunk_of(way, step):
        away = reach - step
        return lax.rem(me_t + (away if way == 0 else n_time - away), n_time)

    def ring_copy(way, step, slot, raw):
        source = grid_ref.at[grid_span(chunk_of(way, step), slot)] if raw else ring.at[way, step - 1, span(slot)]
        return pltpu.make_async_remote_copy(
            src_ref=source,
            dst_ref=ring.at[way, step, span(slot)],
            send_sem=ring_send.at[way, step, slot],
            recv_sem=ring_recv.at[way, step, slot],
            device_id={"tm": neighbour[way]},
            device_id_type=MESH,
        )

    half = pieces // 2

    def open_ring(slot, _):
        ring_copy(0, 0, slot, True).start()
        ring_copy(1, 0, slot + half, True).start()
        return 0

    lax.fori_loop(0, half, open_ring, 0)

    def w_copy(k):
        other = lax.rem(me_t + k, n_time)
        return pltpu.make_async_remote_copy(
            src_ref=wgrid_ref.at[other * n_chan + me_c],
            dst_ref=wparts.at[k],
            send_sem=w_send.at[k],
            recv_sem=w_recv.at[k],
            device_id={"tm": other},
            device_id_type=MESH,
        )

    lax.fori_loop(1, n_time, lambda k, _: (w_copy(k).start(), 0)[1], 0)

    def hop(step, fresh):
        def body(slot, _):
            for way in range(2):
                if fresh[way]:
                    ring_copy(way, step, slot, True).start()
                else:
                    ring_copy(way, step - 1, slot, True).wait_recv()
                    ring[way, step - 1, span(slot)] += grid_ref[grid_span(chunk_of(way, step), slot)]
                    ring_copy(way, step, slot, False).start()
            return 0
        return body

    lax.fori_loop(0, half, hop(1, (False, True)), 0)
    lax.fori_loop(half, pieces, hop(1, (True, False)), 0)
    for step in range(2, reach):
        lax.fori_loop(0, pieces, hop(step, (False, False)), 0)

    def plane_copy(other):
        return pltpu.make_async_remote_copy(
            src_ref=mine.at[other],
            dst_ref=gathered.at[me_c],
            send_sem=plane_send.at[other],
            recv_sem=plane_recv.at[me_c],
            device_id={"chan": other},
            device_id_type=MESH,
        )

    def finish(slot, _):
        for way in range(2):
            ring_copy(way, reach - 1, slot, True).wait_recv()
        where = span(slot)
        mine[where] = grid_ref[grid_span(me_t, slot)] + ring[0, reach - 1, where] + ring[1, reach - 1, where]
        for q in range(per):
            other = lax.rem(slot + turn, pieces) * per + q

            @pl.when(other != me_c)
            def _():
                plane_copy(other).start()

            @pl.when(other == me_c)
            def _():
                gathered[me_c] = mine[me_c]
        return 0

    lax.fori_loop(0, pieces, finish, 0)

    def w_wait(k, _):
        w_copy(k).wait_recv()
        return 0

    lax.fori_loop(1, n_time, w_wait, 0)
    wsum = wgrid_ref[me_t * n_chan + me_c]
    for k in range(1, n_time):
        wsum = wsum + wparts[k]
    for copy in tables:
        copy.wait()
    wcells = jnp.concatenate([jnp.broadcast_to(wsum[a:a + 1], (8, LANES)) for a in range(HALVES)], 1)
    spread_pair = (spread[0], spread[1])
    scale = 1.0 / jnp.maximum(dot3(pair(wcells), spread_pair)[0:1], 1.0)

    def plane_wait(k, _):
        other = lax.rem(me_c + k, n_chan)
        pltpu.make_async_remote_copy(
            src_ref=mine.at[other],
            dst_ref=gathered.at[other],
            send_sem=plane_send.at[other],
            recv_sem=plane_recv.at[other],
            device_id={"chan": other},
            device_id_type=MESH,
        ).wait_recv()
        return 0

    lax.fori_loop(1, n_chan, plane_wait, 0)
    cells = jnp.concatenate(
        [gathered[:, a * rows:(a + 1) * rows, :].reshape(n_chan * rows, LANES) for a in range(HALVES)], 1
    )
    normal = pair(dot3(pair(cells), spread_pair) * scale)
    out_ref[...] = dot3((delay[0], delay[1]), normal)

    def drain_ring(way, step, low, high):
        lax.fori_loop(low, high, lambda slot, _: (ring_copy(way, step, slot, True).wait_send(), 0)[1], 0)

    drain_ring(0, 0, 0, half)
    drain_ring(1, 0, half, pieces)
    for step in range(1, reach):
        for way in range(2):
            drain_ring(way, step, 0, pieces)
    lax.fori_loop(1, n_time, lambda k, _: (w_copy(k).wait_send(), 0)[1], 0)
    lax.fori_loop(1, n_chan, lambda k, _: (plane_copy(lax.rem(me_c + k, n_chan)).wait_send(), 0)[1], 0)


def exchange(grid, wgrid, n_time, n_chan):
    rows2 = grid.shape[1]
    rows = rows2 // HALVES
    total = rows * n_chan
    per = max(1, n_chan // 8)
    pieces = n_chan // per
    reach = n_time // 2
    delay = jnp.asarray(split_bf16(delay_table(total // 2)))
    spread = jnp.asarray(split_bf16(spread_table()))
    vmem = pl.BlockSpec(memory_space=pltpu.VMEM)
    hbm = pl.BlockSpec(memory_space=pl.ANY)
    return pl.pallas_call(
        functools.partial(exchange_kernel, n_time, n_chan, per),
        in_specs=[vmem, vmem, hbm, hbm],
        out_specs=vmem,
        out_shape=jax.ShapeDtypeStruct((total, TILE), jnp.float32),
        scratch_shapes=[
            pltpu.VMEM((2, reach, n_chan, rows2, LANES), jnp.float32),
            pltpu.VMEM((n_chan, rows2, LANES), jnp.float32),
            pltpu.VMEM((n_chan, rows2, LANES), jnp.float32),
            pltpu.VMEM((n_time, 8, LANES), jnp.float32),
            pltpu.VMEM(delay.shape, jnp.bfloat16),
            pltpu.VMEM(spread.shape, jnp.bfloat16),
            pltpu.SemaphoreType.DMA((2, reach, pieces)),
            pltpu.SemaphoreType.DMA((2, reach, pieces)),
            pltpu.SemaphoreType.DMA((n_chan,)),
            pltpu.SemaphoreType.DMA((n_chan,)),
            pltpu.SemaphoreType.DMA((n_time,)),
            pltpu.SemaphoreType.DMA((n_time,)),
            pltpu.SemaphoreType.DMA((2,)),
        ],
        compiler_params=pltpu.CompilerParams(collective_id=0, has_side_effects=True, vmem_limit_bytes=40 << 20),
        name="exchange",
    )(grid, wgrid, delay, spread)


def local(visibilities, vis_weight, tile_index, tile_offset, live_count):
    channels, parts, groups, slots = visibilities.shape
    n_chan = lax.axis_size("chan")
    n_time = lax.axis_size("tm")
    data = visibilities.reshape(channels * parts, groups, slots)
    grid, wgrid = gridding(data, vis_weight, tile_index, tile_offset, live_count.reshape(groups), n_chan * n_time)
    result = exchange(grid, wgrid, n_time, n_chan)
    return result.reshape(2, channels * n_chan, TILE)


def solution(mesh):
    placed = (P("chan", None, "tm", None), P("tm", None), P("tm"), P("tm", None), P("tm", None))
    return jax.shard_map(
        local, mesh=mesh, in_specs=placed, out_specs=P(None, None, ("tm", "chan")), check_vma=False
    )
```

```python
import functools
import math

import jax
import jax.numpy as jnp
import ml_dtypes
import numpy as np
from jax import lax
from jax.experimental import pallas as pl
from jax.experimental.pallas import tpu as pltpu
from jax.sharding import PartitionSpec as P

TSIDE = 16
TILE = TSIDE * TSIDE
LANES = 128
KERNEL_SIGMA2 = 1.44
KERNEL_REACH = 3
HALVES = 2
MESH = pl.DeviceIdType.MESH


def split_bf16(table):
    high = table.astype(ml_dtypes.bfloat16)
    low = (table - high.astype(np.float64)).astype(ml_dtypes.bfloat16)
    return np.stack([high, low])


def spread_table():
    step = np.arange(TSIDE)[:, None] - np.arange(TSIDE)[None, :]
    line = np.where(np.abs(step) <= KERNEL_REACH, np.exp(-step * step / (2.0 * KERNEL_SIGMA2)), 0.0)
    return np.kron(line, line)


def delay_table(channels):
    freq = np.arange(channels)
    angle = 2.0 * np.pi * (freq[:, None] * freq[None, :] % channels) / channels
    phase = 2.0 * np.pi * freq / (channels - 1)
    taper = 0.42323 - 0.49755 * np.cos(phase) + 0.07922 * np.cos(2.0 * phase)
    cos_part = np.cos(angle) * taper[None, :]
    sin_part = np.sin(angle) * taper[None, :]
    upper = np.stack([cos_part, sin_part], axis=-1)
    lower = np.stack([-sin_part, cos_part], axis=-1)
    return np.stack([upper, lower], axis=0).reshape(2 * channels, 2 * channels)


def in_hbm(x):
    return pltpu.with_memory_space_constraint(x, pltpu.HBM)


BATCH = 16
PUSH = 4


def chunks_of(groups):
    cuts = [32, 96, 128]
    if groups < 2 * sum(cuts):
        return [groups]
    rest = groups - sum(cuts)
    return cuts + [rest // 2, rest - rest // 2]


def grid_kernel(
    live_hbm, tile_hbm, vis_hbm, weight_hbm, offset_hbm, grid_ref, wgrid_ref,
    live_ref, tile_ref, vis_ref, weight_ref, offset_ref, vis_sem, small_sem,
):
    rows, groups = vis_ref.shape[:2]
    cuts = chunks_of(groups)
    starts = [sum(cuts[:n]) for n in range(len(cuts))]

    def vis_copy(n):
        part = pl.ds(starts[n], cuts[n])
        return pltpu.make_async_copy(vis_hbm.at[:, part], vis_ref.at[:, part], vis_sem.at[n])

    pairs = [(weight_hbm, weight_ref), (offset_hbm, offset_ref), (live_hbm, live_ref), (tile_hbm, tile_ref)]
    small = [pltpu.make_async_copy(a, b, small_sem.at[n]) for n, (a, b) in enumerate(pairs)]
    vis_copy(0).start()
    for copy in small:
        copy.start()
    for n in range(1, len(cuts)):
        vis_copy(n).start()

    @pl.loop(0, grid_ref.shape[0] // 8)
    def _(i):
        some = pl.ds(i * 8, 8)
        grid_ref[some] = jnp.zeros((8, *grid_ref.shape[1:]), jnp.float32)
        wgrid_ref[some] = jnp.zeros((8, *wgrid_ref.shape[1:]), jnp.float32)

    for copy in small:
        copy.wait()

    cell = lax.broadcasted_iota(jnp.int32, (LANES, LANES), 0).astype(jnp.int16)
    lane = lax.broadcasted_iota(jnp.int32, (8, LANES), 1)
    sub = lax.broadcasted_iota(jnp.int32, (8, LANES), 0)
    zero = jnp.zeros((16, LANES), jnp.bfloat16)
    blank = jnp.zeros((HALVES * rows, LANES), jnp.bfloat16)

    def load(first):
        data = jnp.swapaxes(vis_ref[:, pl.ds(first, BATCH), :].astype(jnp.float32), 0, 1)
        return data, weight_ref[pl.ds(first, BATCH), :].astype(jnp.float32)

    def inner(*acc):
        sums, wsums = acc[:BATCH], acc[BATCH:]

        def feed(first, k, data, weights):
            hots, lefts, highs = [], [], []
            for i in range(PUSH):
                j = PUSH * k + i
                weight = jnp.where(lane < live_ref[0, first + j], jnp.broadcast_to(weights[j:j + 1], (8, LANES)), 0.0)
                offset = jnp.broadcast_to(offset_ref[pl.ds(first + j, 1), :], (8, LANES))
                low = jnp.bitwise_and(offset, LANES - 1)
                high = jnp.right_shift(offset, 7)
                low16 = jnp.concatenate([low, low], 0).astype(jnp.int16)
                weight16 = jnp.concatenate([weight, weight], 0).astype(jnp.bfloat16)
                hots.append(jnp.concatenate(
                    [jnp.where(cell[16 * q:16 * q + 16] == low16, weight16, zero) for q in range(LANES // 16)], 0
                ))
                highs.append(high)
                parts = [
                    jnp.where(high == a, data[j, 8 * q:8 * q + 8], 0.0) for a in range(HALVES) for q in range(rows // 8)
                ]
                left = jnp.concatenate(parts, 0).astype(jnp.bfloat16)
                lefts.append(jnp.concatenate([left, blank] if i % 2 == 0 else [blank, left], 1))
            ones = []
            for i in range(2):
                high = jnp.where(sub < 4, highs[i], highs[i + 2])
                mine = (jnp.bitwise_and(sub, 2) == 2 * i) & (high == jnp.bitwise_and(sub, 1))
                ones.append(jnp.where(mine, 1.0, 0.0))
            wleft = jnp.concatenate([jnp.concatenate(ones, 1), jnp.zeros((8, 2 * LANES), jnp.float32)], 0)
            right = jnp.concatenate([jnp.concatenate(hots[:2], 1), jnp.concatenate(hots[2:], 1)], 0)
            pltpu.matmul_push_rhs(right, k // 2, k % 2, transpose=True)
            for i in range(PUSH):
                pltpu.matmul_acc_lhs(sums[PUSH * k + i], lefts[i], load_staged_rhs=k // 2 if i == 0 else None)
            pltpu.matmul_acc_lhs(wsums[k], wleft.astype(jnp.bfloat16))

        def take(first, k):
            for i in range(PUSH):
                total = pltpu.matmul_pop(sums[PUSH * k + i])
                grid_ref[tile_ref[first + PUSH * k + i]] += total[:, :LANES] if i < 2 else total[:, LANES:]
            total = pltpu.matmul_pop(wsums[k])
            for i in range(PUSH):
                own = total[:8, :LANES] if i < 2 else total[:8, LANES:]
                wgrid_ref[tile_ref[first + PUSH * k + i]] += jnp.where(jnp.right_shift(sub, 1) == i, own, 0.0)

        def body(index, _):
            first = pl.multiple_of(index * BATCH, BATCH)
            data, weights = load(first)
            for k in range(BATCH // PUSH):
                take(first - BATCH, k)
                feed(first, k, data, weights)
            return 0

        vis_copy(0).wait()
        data, weights = load(0)
        for k in range(BATCH // PUSH):
            feed(0, k, data, weights)
        for n in range(len(cuts)):
            if n > 0:
                vis_copy(n).wait()
            low, high = max(1, starts[n] // BATCH), (starts[n] + cuts[n]) // BATCH
            lax.fori_loop(low, high, body, 0, unroll=next((u for u in (8, 4, 3, 2) if (high - low) % u == 0 and high - low > u), 1))
        for k in range(BATCH // PUSH):
            take(groups - BATCH, k)

    def space(unit, depth):
        return pltpu.ACC(unit)((depth, 2 * LANES), jnp.float32)

    pl.run_scoped(
        inner,
        *[space(k % 2, HALVES * rows) for k in range(BATCH // PUSH) for i in range(PUSH)],
        *[space(k % 2, 16) for k in range(BATCH // PUSH)],
    )


def gridding(data, weight, tiles, offset, live, n_tile):
    rows, groups, slots = data.shape
    hbm = pl.BlockSpec(memory_space=pltpu.HBM)
    vmem = pl.BlockSpec(memory_space=pltpu.VMEM)
    return pl.pallas_call(
        grid_kernel,
        in_specs=[hbm] * 5,
        out_specs=[vmem, vmem],
        out_shape=[
            jax.ShapeDtypeStruct((n_tile, HALVES * rows, LANES), jnp.float32),
            jax.ShapeDtypeStruct((n_tile, 8, LANES), jnp.float32),
        ],
        scratch_shapes=[
            pltpu.SMEM(live.shape, jnp.int32),
            pltpu.SMEM(tiles.shape, jnp.int32),
            pltpu.VMEM(data.shape, data.dtype),
            pltpu.VMEM(weight.shape, weight.dtype),
            pltpu.VMEM(offset.shape, jnp.int32),
            pltpu.SemaphoreType.DMA((len(chunks_of(groups)),)),
            pltpu.SemaphoreType.DMA((4,)),
        ],
        compiler_params=pltpu.CompilerParams(vmem_limit_bytes=24 << 20),
        cost_estimate=pl.CostEstimate(flops=2 * groups * rows * slots * TILE, bytes_accessed=data.size * 2, transcendentals=0),
        name="gridding",
    )(*[in_hbm(x) for x in (live, tiles, data, weight, offset)])


def dot3(left, right):
    dot = functools.partial(jnp.dot, preferred_element_type=jnp.float32)
    return dot(left[0], right[0]) + (dot(left[0], right[1]) + dot(left[1], right[0]))


def pair(x):
    high = x.astype(jnp.bfloat16)
    return high, (x - high.astype(jnp.float32)).astype(jnp.bfloat16)


def exchange_kernel(
    n_time, n_chan, per, grid_ref, wgrid_ref, delay_hbm, spread_hbm, out_ref,
    ring, mine, gathered, wparts, delay, spread, scale,
    ring_send, ring_recv, plane_send, plane_recv, w_send, w_recv, table_sem,
):
    me_t = lax.axis_index("tm")
    me_c = lax.axis_index("chan")
    pieces = n_chan // per
    reach = n_time // 2
    rows2 = grid_ref.shape[1]
    rows = rows2 // HALVES
    turn = me_c // per
    neighbour = (lax.rem(me_t + 1, n_time), lax.rem(me_t + n_time - 1, n_time))

    tables = [pltpu.make_async_copy(delay_hbm, delay, table_sem.at[0]),
              pltpu.make_async_copy(spread_hbm, spread, table_sem.at[1])]
    for copy in tables:
        copy.start()

    barrier = pltpu.get_barrier_semaphore()

    def greet_t(k, _):
        pl.semaphore_signal(barrier, inc=1, device_id={"tm": lax.rem(me_t + k, n_time)}, device_id_type=MESH)
        return 0

    def greet_c(k, _):
        pl.semaphore_signal(barrier, inc=1, device_id={"chan": lax.rem(me_c + k, n_chan)}, device_id_type=MESH)
        return 0

    greet_t(1, 0)
    greet_t(n_time - 1, 0)
    lax.fori_loop(2, n_time - 1, greet_t, 0)
    lax.fori_loop(1, n_chan, greet_c, 0)
    pl.semaphore_wait(barrier, n_time - 1 + n_chan - 1)

    def piece_of(slot):
        return lax.rem(slot + turn + 1, pieces)

    def span(slot):
        return pl.ds(piece_of(slot) * per, per)

    def grid_span(chunk, slot):
        return pl.ds(chunk * n_chan + piece_of(slot) * per, per)

    def chunk_of(way, step):
        away = reach - step
        return lax.rem(me_t + (away if way == 0 else n_time - away), n_time)

    def ring_copy(way, step, slot, raw):
        source = grid_ref.at[grid_span(chunk_of(way, step), slot)] if raw else ring.at[way, step - 1, span(slot)]
        return pltpu.make_async_remote_copy(
            src_ref=source,
            dst_ref=ring.at[way, step, span(slot)],
            send_sem=ring_send.at[way, step, slot],
            recv_sem=ring_recv.at[way, step, slot],
            device_id={"tm": neighbour[way]},
            device_id_type=MESH,
        )

    half = pieces // 2

    def open_ring(slot, _):
        ring_copy(0, 0, slot, True).start()
        ring_copy(1, 0, slot + half, True).start()
        return 0

    lax.fori_loop(0, half, open_ring, 0)

    def w_copy(k):
        other = lax.rem(me_t + k, n_time)
        return pltpu.make_async_remote_copy(
            src_ref=wgrid_ref.at[other * n_chan + me_c],
            dst_ref=wparts.at[k],
            send_sem=w_send.at[k],
            recv_sem=w_recv.at[k],
            device_id={"tm": other},
            device_id_type=MESH,
        )

    lax.fori_loop(1, n_time, lambda k, _: (w_copy(k).start(), 0)[1], 0)

    def hop(step, fresh):
        def body(slot, _):
            for way in range(2):
                if fresh[way]:
                    ring_copy(way, step, slot, True).start()
                else:
                    ring_copy(way, step - 1, slot, True).wait_recv()
                    ring[way, step - 1, span(slot)] += grid_ref[grid_span(chunk_of(way, step), slot)]
                    ring_copy(way, step, slot, False).start()
            return 0
        return body

    lax.fori_loop(0, half, hop(1, (False, True)), 0)
    lax.fori_loop(half, pieces, hop(1, (True, False)), 0)
    for step in range(2, reach):
        lax.fori_loop(0, pieces, hop(step, (False, False)), 0)

    def plane_copy(other):
        return pltpu.make_async_remote_copy(
            src_ref=mine.at[other],
            dst_ref=gathered.at[me_c],
            send_sem=plane_send.at[other],
            recv_sem=plane_recv.at[me_c],
            device_id={"chan": other},
            device_id_type=MESH,
        )

    def w_wait(k, _):
        w_copy(k).wait_recv()
        return 0

    lax.fori_loop(1, n_time, w_wait, 0)
    wsum = wgrid_ref[me_t * n_chan + me_c]
    for k in range(1, n_time):
        wsum = wsum + wparts[k]
    for copy in tables:
        copy.wait()
    halves = [sum(wsum[HALVES * i + a:HALVES * i + a + 1] for i in range(PUSH)) for a in range(HALVES)]
    wcells = jnp.concatenate([jnp.broadcast_to(half, (8, LANES)) for half in halves], 1)
    spread_pair = (spread[0], spread[1])
    scale[...] = jnp.broadcast_to(1.0 / jnp.maximum(dot3(pair(wcells), spread_pair), 1.0), scale.shape)

    def finish(slot, _):
        for way in range(2):
            ring_copy(way, reach - 1, slot, True).wait_recv()
        where = span(slot)
        mine[where] = grid_ref[grid_span(me_t, slot)] + ring[0, reach - 1, where] + ring[1, reach - 1, where]
        for q in range(per):
            other = piece_of(slot) * per + q

            @pl.when(other != me_c)
            def _():
                plane_copy(other).start()

            @pl.when(other == me_c)
            def _():
                gathered[me_c] = mine[me_c]
        return 0

    def absorb(slot, first):
        block = lax.rem(turn + pieces - slot - 1 + pieces, pieces)
        for q in range(per):
            other = block * per + q

            @pl.when(other != me_c)
            def _():
                pltpu.make_async_remote_copy(
                    src_ref=mine.at[other],
                    dst_ref=gathered.at[other],
                    send_sem=plane_send.at[other],
                    recv_sem=plane_recv.at[other],
                    device_id={"chan": other},
                    device_id_type=MESH,
                ).wait_recv()

        some = gathered[pl.ds(block * per, per)]
        cells = jnp.concatenate([some[:, a * rows:(a + 1) * rows, :].reshape(per * rows, LANES) for a in range(HALVES)], 1)
        normal = pair(dot3(pair(cells), spread_pair) * scale[0:1])
        part = dot3((delay[0, block], delay[1, block]), normal)
        out_ref[...] = part if first else out_ref[...] + part

    def both(slot, _):
        finish(slot, 0)
        absorb(slot - 1, False)
        return 0

    finish(0, 0)
    finish(1, 0)
    absorb(0, True)
    lax.fori_loop(2, pieces, both, 0)
    absorb(pieces - 1, False)

    def drain_ring(way, step, low, high):
        lax.fori_loop(low, high, lambda slot, _: (ring_copy(way, step, slot, True).wait_send(), 0)[1], 0)

    drain_ring(0, 0, 0, half)
    drain_ring(1, 0, half, pieces)
    for step in range(1, reach):
        for way in range(2):
            drain_ring(way, step, 0, pieces)
    lax.fori_loop(1, n_time, lambda k, _: (w_copy(k).wait_send(), 0)[1], 0)
    lax.fori_loop(1, n_chan, lambda k, _: (plane_copy(lax.rem(me_c + k, n_chan)).wait_send(), 0)[1], 0)


def exchange(grid, wgrid, n_time, n_chan):
    rows2 = grid.shape[1]
    rows = rows2 // HALVES
    total = rows * n_chan
    per = max(1, n_chan // 8)
    pieces = n_chan // per
    reach = n_time // 2
    table = split_bf16(delay_table(total // 2)).reshape(2, total, pieces, per * rows)
    delay = jnp.asarray(np.ascontiguousarray(table.transpose(0, 2, 1, 3)))
    spread = jnp.asarray(split_bf16(spread_table()))
    vmem = pl.BlockSpec(memory_space=pltpu.VMEM)
    hbm = pl.BlockSpec(memory_space=pl.ANY)
    return pl.pallas_call(
        functools.partial(exchange_kernel, n_time, n_chan, per),
        in_specs=[vmem, vmem, hbm, hbm],
        out_specs=vmem,
        out_shape=jax.ShapeDtypeStruct((total, TILE), jnp.float32),
        scratch_shapes=[
            pltpu.VMEM((2, reach, n_chan, rows2, LANES), jnp.float32),
            pltpu.VMEM((n_chan, rows2, LANES), jnp.float32),
            pltpu.VMEM((n_chan, rows2, LANES), jnp.float32),
            pltpu.VMEM((n_time, 8, LANES), jnp.float32),
            pltpu.VMEM(delay.shape, jnp.bfloat16),
            pltpu.VMEM(spread.shape, jnp.bfloat16),
            pltpu.VMEM((8, TILE), jnp.float32),
            pltpu.SemaphoreType.DMA((2, reach, pieces)),
            pltpu.SemaphoreType.DMA((2, reach, pieces)),
            pltpu.SemaphoreType.DMA((n_chan,)),
            pltpu.SemaphoreType.DMA((n_chan,)),
            pltpu.SemaphoreType.DMA((n_time,)),
            pltpu.SemaphoreType.DMA((n_time,)),
            pltpu.SemaphoreType.DMA((2,)),
        ],
        compiler_params=pltpu.CompilerParams(collective_id=0, has_side_effects=True, vmem_limit_bytes=40 << 20),
        name="exchange",
    )(grid, wgrid, in_hbm(delay), in_hbm(spread))


def local(visibilities, vis_weight, tile_index, tile_offset, live_count):
    channels, parts, groups, slots = visibilities.shape
    n_chan = lax.axis_size("chan")
    n_time = lax.axis_size("tm")
    data = visibilities.reshape(channels * parts, groups, slots)
    grid, wgrid = gridding(data, vis_weight, tile_index, tile_offset, live_count, n_chan * n_time)
    result = exchange(grid, wgrid, n_time, n_chan)
    return result.reshape(2, channels * n_chan, TILE)


def solution(mesh):
    placed = (P("chan", None, "tm", None), P("tm", None), P("tm"), P("tm", None), P("tm", None))
    return jax.shard_map(
        local, mesh=mesh, in_specs=placed, out_specs=P(None, None, ("tm", "chan")), check_vma=False
    )
```

```python
import functools
import math

import jax
import jax.numpy as jnp
import ml_dtypes
import numpy as np
from jax import lax
from jax.experimental import pallas as pl
from jax.experimental.pallas import tpu as pltpu
from jax.sharding import PartitionSpec as P

TSIDE = 16
TILE = TSIDE * TSIDE
LANES = 128
KERNEL_SIGMA2 = 1.44
KERNEL_REACH = 3
HALVES = 2
MESH = pl.DeviceIdType.MESH


def split_bf16(table):
    high = table.astype(ml_dtypes.bfloat16)
    low = (table - high.astype(np.float64)).astype(ml_dtypes.bfloat16)
    return np.stack([high, low])


def spread_table():
    step = np.arange(TSIDE)[:, None] - np.arange(TSIDE)[None, :]
    line = np.where(np.abs(step) <= KERNEL_REACH, np.exp(-step * step / (2.0 * KERNEL_SIGMA2)), 0.0)
    return np.kron(line, line)


def delay_table(channels):
    freq = np.arange(channels)
    angle = 2.0 * np.pi * (freq[:, None] * freq[None, :] % channels) / channels
    phase = 2.0 * np.pi * freq / (channels - 1)
    taper = 0.42323 - 0.49755 * np.cos(phase) + 0.07922 * np.cos(2.0 * phase)
    cos_part = np.cos(angle) * taper[None, :]
    sin_part = np.sin(angle) * taper[None, :]
    upper = np.stack([cos_part, sin_part], axis=-1)
    lower = np.stack([-sin_part, cos_part], axis=-1)
    return np.stack([upper, lower], axis=0).reshape(2 * channels, 2 * channels)


def in_hbm(x):
    return pltpu.with_memory_space_constraint(x, pltpu.HBM)


BATCH = 16
PUSH = 4


def chunks_of(groups):
    cuts = [32, 96, 128]
    if groups < 2 * sum(cuts):
        return [groups]
    rest = groups - sum(cuts)
    return cuts + [rest // 2, rest - rest // 2]


def grid_kernel(
    live_hbm, tile_hbm, vis_hbm, weight_hbm, offset_hbm, grid_ref, wgrid_ref,
    live_ref, tile_ref, vis_ref, weight_ref, offset_ref, vis_sem, small_sem,
):
    rows, groups = vis_ref.shape[:2]
    cuts = chunks_of(groups)
    starts = [sum(cuts[:n]) for n in range(len(cuts))]

    def vis_copy(n):
        part = pl.ds(starts[n], cuts[n])
        return pltpu.make_async_copy(vis_hbm.at[:, part], vis_ref.at[:, part], vis_sem.at[n])

    pairs = [(weight_hbm, weight_ref), (offset_hbm, offset_ref), (live_hbm, live_ref), (tile_hbm, tile_ref)]
    small = [pltpu.make_async_copy(a, b, small_sem.at[n]) for n, (a, b) in enumerate(pairs)]
    vis_copy(0).start()
    for copy in small:
        copy.start()
    for n in range(1, len(cuts)):
        vis_copy(n).start()

    @pl.loop(0, grid_ref.shape[0] // 8)
    def _(i):
        some = pl.ds(i * 8, 8)
        grid_ref[some] = jnp.zeros((8, *grid_ref.shape[1:]), jnp.float32)
        wgrid_ref[some] = jnp.zeros((8, *wgrid_ref.shape[1:]), jnp.float32)

    for copy in small:
        copy.wait()

    cell = lax.broadcasted_iota(jnp.int32, (LANES, LANES), 0).astype(jnp.int16)
    lane = lax.broadcasted_iota(jnp.int32, (8, LANES), 1)
    sub = lax.broadcasted_iota(jnp.int32, (8, LANES), 0)
    zero = jnp.zeros((16, LANES), jnp.bfloat16)
    blank = jnp.zeros((HALVES * rows, LANES), jnp.bfloat16)

    def load(first):
        data = jnp.swapaxes(vis_ref[:, pl.ds(first, BATCH), :].astype(jnp.float32), 0, 1)
        return data, weight_ref[pl.ds(first, BATCH), :].astype(jnp.float32)

    def inner(*acc):
        sums, wsums = acc[:BATCH], acc[BATCH:]

        def feed(first, k, data, weights):
            hots, lefts, highs = [], [], []
            for i in range(PUSH):
                j = PUSH * k + i
                weight = jnp.where(lane < live_ref[0, first + j], jnp.broadcast_to(weights[j:j + 1], (8, LANES)), 0.0)
                offset = jnp.broadcast_to(offset_ref[pl.ds(first + j, 1), :], (8, LANES))
                low = jnp.bitwise_and(offset, LANES - 1)
                high = jnp.right_shift(offset, 7)
                low16 = jnp.concatenate([low, low], 0).astype(jnp.int16)
                weight16 = jnp.concatenate([weight, weight], 0).astype(jnp.bfloat16)
                hots.append(jnp.concatenate(
                    [jnp.where(cell[16 * q:16 * q + 16] == low16, weight16, zero) for q in range(LANES // 16)], 0
                ))
                highs.append(high)
                parts = [
                    jnp.where(high == a, data[j, 8 * q:8 * q + 8], 0.0) for a in range(HALVES) for q in range(rows // 8)
                ]
                left = jnp.concatenate(parts, 0).astype(jnp.bfloat16)
                lefts.append(jnp.concatenate([left, blank] if i % 2 == 0 else [blank, left], 1))
            ones = []
            for i in range(2):
                high = jnp.where(sub < 4, highs[i], highs[i + 2])
                mine = (jnp.bitwise_and(sub, 2) == 2 * i) & (high == jnp.bitwise_and(sub, 1))
                ones.append(jnp.where(mine, 1.0, 0.0))
            wleft = jnp.concatenate([jnp.concatenate(ones, 1), jnp.zeros((8, 2 * LANES), jnp.float32)], 0)
            right = jnp.concatenate([jnp.concatenate(hots[:2], 1), jnp.concatenate(hots[2:], 1)], 0)
            pltpu.matmul_push_rhs(right, k // 2, k % 2, transpose=True)
            for i in range(PUSH):
                pltpu.matmul_acc_lhs(sums[PUSH * k + i], lefts[i], load_staged_rhs=k // 2 if i == 0 else None)
            pltpu.matmul_acc_lhs(wsums[k], wleft.astype(jnp.bfloat16))

        def take(first, k):
            for i in range(PUSH):
                total = pltpu.matmul_pop(sums[PUSH * k + i])
                grid_ref[tile_ref[first + PUSH * k + i]] += total[:, :LANES] if i < 2 else total[:, LANES:]
            total = pltpu.matmul_pop(wsums[k])
            for i in range(PUSH):
                own = total[:8, :LANES] if i < 2 else total[:8, LANES:]
                wgrid_ref[tile_ref[first + PUSH * k + i]] += jnp.where(jnp.right_shift(sub, 1) == i, own, 0.0)

        def body(index, _):
            first = pl.multiple_of(index * BATCH, BATCH)
            data, weights = load(first)
            for k in range(BATCH // PUSH):
                take(first - BATCH, k)
                feed(first, k, data, weights)
            return 0

        vis_copy(0).wait()
        data, weights = load(0)
        for k in range(BATCH // PUSH):
            feed(0, k, data, weights)
        for n in range(len(cuts)):
            if n > 0:
                vis_copy(n).wait()
            low, high = max(1, starts[n] // BATCH), (starts[n] + cuts[n]) // BATCH
            lax.fori_loop(low, high, body, 0, unroll=next((u for u in (8, 4, 3, 2) if (high - low) % u == 0 and high - low > u), 1))
        for k in range(BATCH // PUSH):
            take(groups - BATCH, k)

    def space(unit, depth):
        return pltpu.ACC(unit)((depth, 2 * LANES), jnp.float32)

    pl.run_scoped(
        inner,
        *[space(k % 2, HALVES * rows) for k in range(BATCH // PUSH) for i in range(PUSH)],
        *[space(k % 2, 16) for k in range(BATCH // PUSH)],
    )


def gridding(data, weight, tiles, offset, live, n_tile):
    rows, groups, slots = data.shape
    hbm = pl.BlockSpec(memory_space=pltpu.HBM)
    vmem = pl.BlockSpec(memory_space=pltpu.VMEM)
    return pl.pallas_call(
        grid_kernel,
        in_specs=[hbm] * 5,
        out_specs=[vmem, vmem],
        out_shape=[
            jax.ShapeDtypeStruct((n_tile, HALVES * rows, LANES), jnp.float32),
            jax.ShapeDtypeStruct((n_tile, 8, LANES), jnp.float32),
        ],
        scratch_shapes=[
            pltpu.SMEM(live.shape, jnp.int32),
            pltpu.SMEM(tiles.shape, jnp.int32),
            pltpu.VMEM(data.shape, data.dtype),
            pltpu.VMEM(weight.shape, weight.dtype),
            pltpu.VMEM(offset.shape, jnp.int32),
            pltpu.SemaphoreType.DMA((len(chunks_of(groups)),)),
            pltpu.SemaphoreType.DMA((4,)),
        ],
        compiler_params=pltpu.CompilerParams(vmem_limit_bytes=24 << 20),
        cost_estimate=pl.CostEstimate(flops=2 * groups * rows * slots * TILE, bytes_accessed=data.size * 2, transcendentals=0),
        name="gridding",
    )(*[in_hbm(x) for x in (live, tiles, data, weight, offset)])


def dot3(left, right):
    dot = functools.partial(jnp.dot, preferred_element_type=jnp.float32)
    return dot(left[0], right[0]) + (dot(left[0], right[1]) + dot(left[1], right[0]))


def pair(x):
    high = x.astype(jnp.bfloat16)
    return high, (x - high.astype(jnp.float32)).astype(jnp.bfloat16)


def exchange_kernel(
    n_time, n_chan, per, grid_ref, wgrid_ref, delay_hbm, spread_hbm, out_ref,
    ring, mine, gathered, wown, wparts, delay, spread, scale,
    ring_send, ring_recv, plane_send, plane_recv, w_send, w_recv, table_sem,
):
    me_t = lax.axis_index("tm")
    me_c = lax.axis_index("chan")
    pieces = n_chan // per
    wide = pieces // 2
    reach = n_time // 2
    last = reach - 1
    rows2 = grid_ref.shape[1]
    rows = rows2 // HALVES
    turn = me_c // per
    neighbour = (lax.rem(me_t + 1, n_time), lax.rem(me_t + n_time - 1, n_time))

    tables = [pltpu.make_async_copy(delay_hbm, delay, table_sem.at[0]),
              pltpu.make_async_copy(spread_hbm, spread, table_sem.at[1])]
    for copy in tables:
        copy.start()

    barrier = pltpu.get_barrier_semaphore()

    def greet_t(k, _):
        pl.semaphore_signal(barrier, inc=1, device_id={"tm": lax.rem(me_t + k, n_time)}, device_id_type=MESH)
        return 0

    def greet_c(k, _):
        pl.semaphore_signal(barrier, inc=1, device_id={"chan": lax.rem(me_c + k, n_chan)}, device_id_type=MESH)
        return 0

    greet_t(1, 0)
    greet_t(n_time - 1, 0)
    lax.fori_loop(2, n_time - 1, greet_t, 0)
    lax.fori_loop(1, n_chan, greet_c, 0)

    for t in range(n_time):
        part = wgrid_ref[t * n_chan + me_c]
        total = part[0:HALVES]
        for i in range(1, PUSH):
            total = total + part[HALVES * i:HALVES * (i + 1)]
        wown[t, 0:HALVES] = total

    pl.semaphore_wait(barrier, n_time - 1 + n_chan - 1)

    def pair_of(slot):
        return lax.rem(slot + turn // 2 + 1, wide)

    def piece_of(slot):
        return 2 * pair_of(slot // 2) + lax.rem(slot + turn + 1, 2)

    def span(step, slot):
        if step < last:
            return pl.ds(pair_of(slot) * (2 * per), 2 * per)
        return pl.ds(piece_of(slot) * per, per)

    def grid_span(chunk, step, slot):
        if step < last:
            return pl.ds(chunk * n_chan + pair_of(slot) * (2 * per), 2 * per)
        return pl.ds(chunk * n_chan + piece_of(slot) * per, per)

    def chunk_of(way, step):
        away = reach - step
        return lax.rem(me_t + (away if way == 0 else n_time - away), n_time)

    def ring_copy(way, step, slot, raw):
        where = span(step, slot)
        source = grid_ref.at[grid_span(chunk_of(way, step), step, slot)] if raw else ring.at[way, step - 1, where]
        return pltpu.make_async_remote_copy(
            src_ref=source,
            dst_ref=ring.at[way, step, where],
            send_sem=ring_send.at[way, step, slot],
            recv_sem=ring_recv.at[way, step, slot],
            device_id={"tm": neighbour[way]},
            device_id_type=MESH,
        )

    half = wide // 2

    def open_ring(slot, _):
        ring_copy(0, 0, slot, True).start()
        ring_copy(1, 0, slot + half, True).start()
        return 0

    lax.fori_loop(0, half, open_ring, 0)

    def w_copy(k):
        other = lax.rem(me_t + k, n_time)
        return pltpu.make_async_remote_copy(
            src_ref=wown.at[other, pl.ds(0, HALVES)],
            dst_ref=wparts.at[k, pl.ds(0, HALVES)],
            send_sem=w_send.at[k],
            recv_sem=w_recv.at[k],
            device_id={"tm": other},
            device_id_type=MESH,
        )

    lax.fori_loop(1, n_time, lambda k, _: (w_copy(k).start(), 0)[1], 0)

    def hop(step, fresh):
        def body(slot, _):
            for way in range(2):
                if not fresh[way]:
                    ring_copy(way, step - 1, slot, True).wait_recv()
                    ring[way, step - 1, span(step - 1, slot)] += grid_ref[grid_span(chunk_of(way, step), step - 1, slot)]
                if step < last:
                    ring_copy(way, step, slot, fresh[way]).start()
            if step == last:
                for q in range(2):
                    for way in range(2):
                        ring_copy(way, step, 2 * slot + q, fresh[way]).start()
            return 0
        return body

    lax.fori_loop(0, half, hop(1, (False, True)), 0)
    lax.fori_loop(half, wide, hop(1, (True, False)), 0)
    for step in range(2, reach):
        lax.fori_loop(0, wide, hop(step, (False, False)), 0)

    def plane_copy(other):
        return pltpu.make_async_remote_copy(
            src_ref=mine.at[other],
            dst_ref=gathered.at[me_c],
            send_sem=plane_send.at[other],
            recv_sem=plane_recv.at[me_c],
            device_id={"chan": other},
            device_id_type=MESH,
        )

    lax.fori_loop(1, n_time, lambda k, _: (w_copy(k).wait_recv(), 0)[1], 0)
    wsum = wown[me_t, 0:HALVES]
    for k in range(1, n_time):
        wsum = wsum + wparts[k, 0:HALVES]
    for copy in tables:
        copy.wait()
    wcells = jnp.concatenate([jnp.broadcast_to(wsum[a:a + 1], (8, LANES)) for a in range(HALVES)], 1)
    spread_pair = (spread[0], spread[1])
    scale[...] = jnp.broadcast_to(1.0 / jnp.maximum(dot3(pair(wcells), spread_pair), 1.0), scale.shape)

    def finish(slot, _):
        for way in range(2):
            ring_copy(way, last, slot, True).wait_recv()
        where = span(last, slot)
        mine[where] = grid_ref[grid_span(me_t, last, slot)] + ring[0, last, where] + ring[1, last, where]
        for q in range(per):
            other = piece_of(slot) * per + q

            @pl.when(other != me_c)
            def _():
                plane_copy(other).start()

            @pl.when(other == me_c)
            def _():
                gathered[me_c] = mine[me_c]
        return 0

    def absorb(slot, first):
        block = 2 * lax.rem(turn // 2 + pieces - slot // 2 - 1, wide) + lax.rem(turn + pieces - slot - 1, 2)
        for q in range(per):
            other = block * per + q

            @pl.when(other != me_c)
            def _():
                pltpu.make_async_remote_copy(
                    src_ref=mine.at[other],
                    dst_ref=gathered.at[other],
                    send_sem=plane_send.at[other],
                    recv_sem=plane_recv.at[other],
                    device_id={"chan": other},
                    device_id_type=MESH,
                ).wait_recv()

        some = gathered[pl.ds(block * per, per)]
        cells = jnp.concatenate([some[:, a * rows:(a + 1) * rows, :].reshape(per * rows, LANES) for a in range(HALVES)], 1)
        normal = pair(dot3(pair(cells), spread_pair) * scale[0:1])
        part = dot3((delay[0, block], delay[1, block]), normal)
        out_ref[...] = part if first else out_ref[...] + part

    lag = min(3, pieces - 1)

    def both(slot, _):
        finish(slot, 0)
        absorb(slot - lag, False)
        return 0

    lax.fori_loop(0, lag + 1, finish, 0)
    absorb(0, True)
    lax.fori_loop(lag + 1, pieces, both, 0)

    def drain_ring(way, step, low, high):
        lax.fori_loop(low, high, lambda slot, _: (ring_copy(way, step, slot, True).wait_send(), 0)[1], 0)

    drain_ring(0, 0, 0, half)
    drain_ring(1, 0, half, wide)
    for step in range(1, reach):
        for way in range(2):
            drain_ring(way, step, 0, wide if step < last else pieces)
    lax.fori_loop(1, n_time, lambda k, _: (w_copy(k).wait_send(), 0)[1], 0)

    lax.fori_loop(pieces - lag, pieces, lambda k, _: (absorb(k, False), 0)[1], 0)
    lax.fori_loop(1, n_chan, lambda k, _: (plane_copy(lax.rem(me_c + k, n_chan)).wait_send(), 0)[1], 0)


def exchange(grid, wgrid, n_time, n_chan):
    rows2 = grid.shape[1]
    rows = rows2 // HALVES
    total = rows * n_chan
    per = max(1, n_chan // 8)
    pieces = n_chan // per
    reach = n_time // 2
    table = split_bf16(delay_table(total // 2)).reshape(2, total, pieces, per * rows)
    delay = jnp.asarray(np.ascontiguousarray(table.transpose(0, 2, 1, 3)))
    spread = jnp.asarray(split_bf16(spread_table()))
    vmem = pl.BlockSpec(memory_space=pltpu.VMEM)
    hbm = pl.BlockSpec(memory_space=pl.ANY)
    return pl.pallas_call(
        functools.partial(exchange_kernel, n_time, n_chan, per),
        in_specs=[vmem, vmem, hbm, hbm],
        out_specs=vmem,
        out_shape=jax.ShapeDtypeStruct((total, TILE), jnp.float32),
        scratch_shapes=[
            pltpu.VMEM((2, reach, n_chan, rows2, LANES), jnp.float32),
            pltpu.VMEM((n_chan, rows2, LANES), jnp.float32),
            pltpu.VMEM((n_chan, rows2, LANES), jnp.float32),
            pltpu.VMEM((n_time, 8, LANES), jnp.float32),
            pltpu.VMEM((n_time, 8, LANES), jnp.float32),
            pltpu.VMEM(delay.shape, jnp.bfloat16),
            pltpu.VMEM(spread.shape, jnp.bfloat16),
            pltpu.VMEM((8, TILE), jnp.float32),
            pltpu.SemaphoreType.DMA((2, reach, pieces)),
            pltpu.SemaphoreType.DMA((2, reach, pieces)),
            pltpu.SemaphoreType.DMA((n_chan,)),
            pltpu.SemaphoreType.DMA((n_chan,)),
            pltpu.SemaphoreType.DMA((n_time,)),
            pltpu.SemaphoreType.DMA((n_time,)),
            pltpu.SemaphoreType.DMA((2,)),
        ],
        compiler_params=pltpu.CompilerParams(collective_id=0, has_side_effects=True, vmem_limit_bytes=40 << 20),
        name="exchange",
    )(grid, wgrid, in_hbm(delay), in_hbm(spread))


def local(visibilities, vis_weight, tile_index, tile_offset, live_count):
    channels, parts, groups, slots = visibilities.shape
    n_chan = lax.axis_size("chan")
    n_time = lax.axis_size("tm")
    data = visibilities.reshape(channels * parts, groups, slots)
    grid, wgrid = gridding(data, vis_weight, tile_index, tile_offset, live_count, n_chan * n_time)
    result = exchange(grid, wgrid, n_time, n_chan)
    return result.reshape(2, channels * n_chan, TILE)


def solution(mesh):
    placed = (P("chan", None, "tm", None), P("tm", None), P("tm"), P("tm", None), P("tm", None))
    return jax.shard_map(
        local, mesh=mesh, in_specs=placed, out_specs=P(None, None, ("tm", "chan")), check_vma=False
    )
```

```python
import functools
import math

import jax
import jax.numpy as jnp
import ml_dtypes
import numpy as np
from jax import lax
from jax.experimental import pallas as pl
from jax.experimental.pallas import tpu as pltpu
from jax.sharding import PartitionSpec as P

TSIDE = 16
TILE = TSIDE * TSIDE
LANES = 128
KERNEL_SIGMA2 = 1.44
KERNEL_REACH = 3
HALVES = 2
MESH = pl.DeviceIdType.MESH


def split_bf16(table):
    high = table.astype(ml_dtypes.bfloat16)
    low = (table - high.astype(np.float64)).astype(ml_dtypes.bfloat16)
    return np.stack([high, low])


def spread_table():
    step = np.arange(TSIDE)[:, None] - np.arange(TSIDE)[None, :]
    line = np.where(np.abs(step) <= KERNEL_REACH, np.exp(-step * step / (2.0 * KERNEL_SIGMA2)), 0.0)
    return np.kron(line, line)


def delay_table(channels):
    freq = np.arange(channels)
    angle = 2.0 * np.pi * (freq[:, None] * freq[None, :] % channels) / channels
    phase = 2.0 * np.pi * freq / (channels - 1)
    taper = 0.42323 - 0.49755 * np.cos(phase) + 0.07922 * np.cos(2.0 * phase)
    cos_part = np.cos(angle) * taper[None, :]
    sin_part = np.sin(angle) * taper[None, :]
    upper = np.stack([cos_part, sin_part], axis=-1)
    lower = np.stack([-sin_part, cos_part], axis=-1)
    return np.stack([upper, lower], axis=0).reshape(2 * channels, 2 * channels)


def in_hbm(x):
    return pltpu.with_memory_space_constraint(x, pltpu.HBM)


BATCH = 16
PUSH = 4


def chunks_of(groups):
    cuts = [32, 96, 128]
    if groups < 2 * sum(cuts):
        return [groups]
    rest = groups - sum(cuts)
    return cuts + [rest // 2, rest - rest // 2]


def grid_kernel(
    live_hbm, tile_hbm, vis_hbm, weight_hbm, offset_hbm, grid_ref, wgrid_ref,
    live_ref, tile_ref, vis_ref, weight_ref, offset_ref, vis_sem, small_sem,
):
    rows, groups = vis_ref.shape[:2]
    cuts = chunks_of(groups)
    starts = [sum(cuts[:n]) for n in range(len(cuts))]

    def vis_copy(n):
        part = pl.ds(starts[n], cuts[n])
        return pltpu.make_async_copy(vis_hbm.at[:, part], vis_ref.at[:, part], vis_sem.at[n])

    pairs = [(weight_hbm, weight_ref), (offset_hbm, offset_ref), (live_hbm, live_ref), (tile_hbm, tile_ref)]
    small = [pltpu.make_async_copy(a, b, small_sem.at[n]) for n, (a, b) in enumerate(pairs)]
    vis_copy(0).start()
    for copy in small:
        copy.start()
    for n in range(1, len(cuts)):
        vis_copy(n).start()

    @pl.loop(0, grid_ref.shape[0] // 8)
    def _(i):
        some = pl.ds(i * 8, 8)
        grid_ref[some] = jnp.zeros((8, *grid_ref.shape[1:]), jnp.float32)
        wgrid_ref[some] = jnp.zeros((8, *wgrid_ref.shape[1:]), jnp.float32)

    for copy in small:
        copy.wait()

    cell = lax.broadcasted_iota(jnp.int32, (LANES, LANES), 0).astype(jnp.int16)
    lane = lax.broadcasted_iota(jnp.int32, (8, LANES), 1)
    sub = lax.broadcasted_iota(jnp.int32, (8, LANES), 0)
    zero = jnp.zeros((16, LANES), jnp.bfloat16)
    blank = jnp.zeros((HALVES * rows, LANES), jnp.bfloat16)

    def load(first):
        data = jnp.swapaxes(vis_ref[:, pl.ds(first, BATCH), :].astype(jnp.float32), 0, 1)
        return data, weight_ref[pl.ds(first, BATCH), :].astype(jnp.float32)

    def inner(*acc):
        sums, wsums = acc[:BATCH], acc[BATCH:]

        def feed(first, k, data, weights):
            hots, lefts, highs = [], [], []
            for i in range(PUSH):
                j = PUSH * k + i
                weight = jnp.where(lane < live_ref[0, first + j], jnp.broadcast_to(weights[j:j + 1], (8, LANES)), 0.0)
                offset = jnp.broadcast_to(offset_ref[pl.ds(first + j, 1), :], (8, LANES))
                low = jnp.bitwise_and(offset, LANES - 1)
                high = jnp.right_shift(offset, 7)
                low16 = jnp.concatenate([low, low], 0).astype(jnp.int16)
                weight16 = jnp.concatenate([weight, weight], 0).astype(jnp.bfloat16)
                hots.append(jnp.concatenate(
                    [jnp.where(cell[16 * q:16 * q + 16] == low16, weight16, zero) for q in range(LANES // 16)], 0
                ))
                highs.append(high)
                parts = [
                    jnp.where(high == a, data[j, 8 * q:8 * q + 8], 0.0) for a in range(HALVES) for q in range(rows // 8)
                ]
                left = jnp.concatenate(parts, 0).astype(jnp.bfloat16)
                lefts.append(jnp.concatenate([left, blank] if i % 2 == 0 else [blank, left], 1))
            ones = []
            for i in range(2):
                high = jnp.where(sub < 4, highs[i], highs[i + 2])
                mine = (jnp.bitwise_and(sub, 2) == 2 * i) & (high == jnp.bitwise_and(sub, 1))
                ones.append(jnp.where(mine, 1.0, 0.0))
            wleft = jnp.concatenate([jnp.concatenate(ones, 1), jnp.zeros((8, 2 * LANES), jnp.float32)], 0)
            turned = k >= BATCH // PUSH // 2
            if turned:
                hots = [hots[i].T for i in (0, 2, 1, 3)]
            right = jnp.concatenate([jnp.concatenate(hots[:2], 1), jnp.concatenate(hots[2:], 1)], 0)
            pltpu.matmul_push_rhs(right, k // 2, k % 2, transpose=not turned)
            for i in range(PUSH):
                pltpu.matmul_acc_lhs(sums[PUSH * k + i], lefts[i], load_staged_rhs=k // 2 if i == 0 else None)
            pltpu.matmul_acc_lhs(wsums[k], wleft.astype(jnp.bfloat16))

        def take(first, k):
            for i in range(PUSH):
                total = pltpu.matmul_pop(sums[PUSH * k + i])
                grid_ref[tile_ref[first + PUSH * k + i]] += total[:, :LANES] if i < 2 else total[:, LANES:]
            total = pltpu.matmul_pop(wsums[k])
            for i in range(PUSH):
                own = total[:8, :LANES] if i < 2 else total[:8, LANES:]
                wgrid_ref[tile_ref[first + PUSH * k + i]] += jnp.where(jnp.right_shift(sub, 1) == i, own, 0.0)

        def body(index, _):
            first = pl.multiple_of(index * BATCH, BATCH)
            data, weights = load(first)
            for k in range(BATCH // PUSH):
                take(first - BATCH, k)
                feed(first, k, data, weights)
            return 0

        vis_copy(0).wait()
        data, weights = load(0)
        for k in range(BATCH // PUSH):
            feed(0, k, data, weights)
        for n in range(len(cuts)):
            if n > 0:
                vis_copy(n).wait()
            low, high = max(1, starts[n] // BATCH), (starts[n] + cuts[n]) // BATCH
            lax.fori_loop(low, high, body, 0, unroll=next((u for u in (8, 4, 3, 2) if (high - low) % u == 0 and high - low > u), 1))
        for k in range(BATCH // PUSH):
            take(groups - BATCH, k)

    def space(unit, depth):
        return pltpu.ACC(unit)((depth, 2 * LANES), jnp.float32)

    pl.run_scoped(
        inner,
        *[space(k % 2, HALVES * rows) for k in range(BATCH // PUSH) for i in range(PUSH)],
        *[space(k % 2, 16) for k in range(BATCH // PUSH)],
    )


def gridding(data, weight, tiles, offset, live, n_tile):
    rows, groups, slots = data.shape
    hbm = pl.BlockSpec(memory_space=pltpu.HBM)
    vmem = pl.BlockSpec(memory_space=pltpu.VMEM)
    return pl.pallas_call(
        grid_kernel,
        in_specs=[hbm] * 5,
        out_specs=[vmem, vmem],
        out_shape=[
            jax.ShapeDtypeStruct((n_tile, HALVES * rows, LANES), jnp.float32),
            jax.ShapeDtypeStruct((n_tile, 8, LANES), jnp.float32),
        ],
        scratch_shapes=[
            pltpu.SMEM(live.shape, jnp.int32),
            pltpu.SMEM(tiles.shape, jnp.int32),
            pltpu.VMEM(data.shape, data.dtype),
            pltpu.VMEM(weight.shape, weight.dtype),
            pltpu.VMEM(offset.shape, jnp.int32),
            pltpu.SemaphoreType.DMA((len(chunks_of(groups)),)),
            pltpu.SemaphoreType.DMA((4,)),
        ],
        compiler_params=pltpu.CompilerParams(vmem_limit_bytes=24 << 20),
        cost_estimate=pl.CostEstimate(flops=2 * groups * rows * slots * TILE, bytes_accessed=data.size * 2, transcendentals=0),
        name="gridding",
    )(*[in_hbm(x) for x in (live, tiles, data, weight, offset)])


def dot3(left, right):
    dot = functools.partial(jnp.dot, preferred_element_type=jnp.float32)
    return dot(left[0], right[0]) + (dot(left[0], right[1]) + dot(left[1], right[0]))


def pair(x):
    high = x.astype(jnp.bfloat16)
    return high, (x - high.astype(jnp.float32)).astype(jnp.bfloat16)


def exchange_kernel(
    n_time, n_chan, per, grid_ref, wgrid_ref, delay_hbm, spread_hbm, out_ref,
    ring, mine, gathered, wown, wparts, delay, spread, scale,
    ring_send, ring_recv, plane_send, plane_recv, w_send, w_recv, table_sem,
):
    me_t = lax.axis_index("tm")
    me_c = lax.axis_index("chan")
    pieces = n_chan // per
    wide = pieces // 2
    reach = n_time // 2
    last = reach - 1
    fine = 2 if per % 2 == 0 else 1
    rows2 = grid_ref.shape[1]
    rows = rows2 // HALVES
    turn = me_c // per
    neighbour = (lax.rem(me_t + 1, n_time), lax.rem(me_t + n_time - 1, n_time))

    tables = [pltpu.make_async_copy(delay_hbm, delay, table_sem.at[0]),
              pltpu.make_async_copy(spread_hbm, spread, table_sem.at[1])]
    for copy in tables:
        copy.start()

    barrier = pltpu.get_barrier_semaphore()

    def greet_t(k, _):
        pl.semaphore_signal(barrier, inc=1, device_id={"tm": lax.rem(me_t + k, n_time)}, device_id_type=MESH)
        return 0

    def greet_c(k, _):
        pl.semaphore_signal(barrier, inc=1, device_id={"chan": lax.rem(me_c + k, n_chan)}, device_id_type=MESH)
        return 0

    greet_t(1, 0)
    greet_t(n_time - 1, 0)
    lax.fori_loop(2, n_time - 1, greet_t, 0)
    lax.fori_loop(1, n_chan, greet_c, 0)

    pl.semaphore_wait(barrier, n_time - 1 + n_chan - 1)

    def pair_of(slot):
        return lax.rem(slot + turn // 2 + 1, wide)

    def piece_of(slot):
        return 2 * pair_of(slot // 2) + lax.rem(slot + turn + 1, 2)

    def span(step, slot):
        if step < last:
            return pl.ds(pair_of(slot) * (2 * per), 2 * per)
        return pl.ds(piece_of(slot // fine) * per + lax.rem(slot, fine) * (per // fine), per // fine)

    def grid_span(chunk, step, slot):
        if step < last:
            return pl.ds(chunk * n_chan + pair_of(slot) * (2 * per), 2 * per)
        return pl.ds(chunk * n_chan + piece_of(slot // fine) * per + lax.rem(slot, fine) * (per // fine), per // fine)

    def chunk_of(way, step):
        away = reach - step
        return lax.rem(me_t + (away if way == 0 else n_time - away), n_time)

    def ring_copy(way, step, slot, raw):
        where = span(step, slot)
        source = grid_ref.at[grid_span(chunk_of(way, step), step, slot)] if raw else ring.at[way, step - 1, where]
        return pltpu.make_async_remote_copy(
            src_ref=source,
            dst_ref=ring.at[way, step, where],
            send_sem=ring_send.at[way, step, slot],
            recv_sem=ring_recv.at[way, step, slot],
            device_id={"tm": neighbour[way]},
            device_id_type=MESH,
        )

    half = wide // 2

    def open_ring(slot, _):
        ring_copy(0, 0, slot, True).start()
        ring_copy(1, 0, slot + half, True).start()
        return 0

    lax.fori_loop(0, half, open_ring, 0)

    for t in range(n_time):
        part = wgrid_ref[t * n_chan + me_c]
        total = part[0:HALVES]
        for i in range(1, PUSH):
            total = total + part[HALVES * i:HALVES * (i + 1)]
        wown[t, 0:HALVES] = total

    def w_copy(k):
        other = lax.rem(me_t + k, n_time)
        return pltpu.make_async_remote_copy(
            src_ref=wown.at[other, pl.ds(0, HALVES)],
            dst_ref=wparts.at[k, pl.ds(0, HALVES)],
            send_sem=w_send.at[k],
            recv_sem=w_recv.at[k],
            device_id={"tm": other},
            device_id_type=MESH,
        )

    lax.fori_loop(1, n_time, lambda k, _: (w_copy(k).start(), 0)[1], 0)

    def hop(step, fresh):
        def body(slot, _):
            for way in range(2):
                if not fresh[way]:
                    ring_copy(way, step - 1, slot, True).wait_recv()
                    ring[way, step - 1, span(step - 1, slot)] += grid_ref[grid_span(chunk_of(way, step), step - 1, slot)]
                if step < last:
                    ring_copy(way, step, slot, fresh[way]).start()
            if step == last:
                for q in range(2 * fine):
                    for way in range(2):
                        ring_copy(way, step, 2 * fine * slot + q, fresh[way]).start()
            return 0
        return body

    lax.fori_loop(0, half, hop(1, (False, True)), 0)
    lax.fori_loop(half, wide, hop(1, (True, False)), 0)
    for step in range(2, reach):
        lax.fori_loop(0, wide, hop(step, (False, False)), 0)

    def plane_copy(other):
        return pltpu.make_async_remote_copy(
            src_ref=mine.at[other],
            dst_ref=gathered.at[me_c],
            send_sem=plane_send.at[other],
            recv_sem=plane_recv.at[me_c],
            device_id={"chan": other},
            device_id_type=MESH,
        )

    lax.fori_loop(1, n_time, lambda k, _: (w_copy(k).wait_recv(), 0)[1], 0)
    wsum = wown[me_t, 0:HALVES]
    for k in range(1, n_time):
        wsum = wsum + wparts[k, 0:HALVES]
    for copy in tables:
        copy.wait()
    wcells = jnp.concatenate([jnp.broadcast_to(wsum[a:a + 1], (8, LANES)) for a in range(HALVES)], 1)
    spread_pair = (spread[0], spread[1])
    scale[...] = jnp.broadcast_to(1.0 / jnp.maximum(dot3(pair(wcells), spread_pair), 1.0), scale.shape)

    def finish(slot, _):
        for way in range(2):
            ring_copy(way, last, slot, True).wait_recv()
        where = span(last, slot)
        mine[where] = grid_ref[grid_span(me_t, last, slot)] + ring[0, last, where] + ring[1, last, where]
        for q in range(per // fine):
            other = piece_of(slot // fine) * per + lax.rem(slot, fine) * (per // fine) + q

            @pl.when(other != me_c)
            def _():
                plane_copy(other).start()

            @pl.when(other == me_c)
            def _():
                gathered[me_c] = mine[me_c]
        return 0

    def absorb(slot, first):
        block = 2 * lax.rem(turn // 2 + pieces - slot // 2 - 1, wide) + lax.rem(turn + pieces - slot - 1, 2)
        for q in range(per):
            other = block * per + q

            @pl.when(other != me_c)
            def _():
                pltpu.make_async_remote_copy(
                    src_ref=mine.at[other],
                    dst_ref=gathered.at[other],
                    send_sem=plane_send.at[other],
                    recv_sem=plane_recv.at[other],
                    device_id={"chan": other},
                    device_id_type=MESH,
                ).wait_recv()

        some = gathered[pl.ds(block * per, per)]
        cells = jnp.concatenate([some[:, a * rows:(a + 1) * rows, :].reshape(per * rows, LANES) for a in range(HALVES)], 1)
        normal = dot3(pair(cells), spread_pair) * scale[0:1]
        high, low = pair(normal)
        part = jnp.dot(delay[block], jnp.concatenate([high, high, low], 0), preferred_element_type=jnp.float32)
        out_ref[...] = part if first else out_ref[...] + part

    lag = min(3, pieces - 1)

    def both(slot, _):
        for f in range(fine):
            finish(slot * fine + f, 0)
        absorb(slot - lag, False)
        return 0

    lax.fori_loop(0, (lag + 1) * fine, finish, 0)
    absorb(0, True)
    lax.fori_loop(lag + 1, pieces, both, 0)

    def drain_ring(way, step, low, high):
        lax.fori_loop(low, high, lambda slot, _: (ring_copy(way, step, slot, True).wait_send(), 0)[1], 0)

    drain_ring(0, 0, 0, half)
    drain_ring(1, 0, half, wide)
    for step in range(1, reach):
        for way in range(2):
            drain_ring(way, step, 0, wide if step < last else pieces * fine)
    lax.fori_loop(1, n_time, lambda k, _: (w_copy(k).wait_send(), 0)[1], 0)

    lax.fori_loop(pieces - lag, pieces, lambda k, _: (absorb(k, False), 0)[1], 0)
    lax.fori_loop(1, n_chan, lambda k, _: (plane_copy(lax.rem(me_c + k, n_chan)).wait_send(), 0)[1], 0)


def exchange(grid, wgrid, n_time, n_chan):
    rows2 = grid.shape[1]
    rows = rows2 // HALVES
    total = rows * n_chan
    per = max(1, n_chan // 8)
    pieces = n_chan // per
    reach = n_time // 2
    table = split_bf16(delay_table(total // 2)).reshape(2, total, pieces, per * rows)
    delay = jnp.asarray(np.concatenate([table[0], table[1], table[0]], -1).transpose(1, 0, 2))
    spread = jnp.asarray(split_bf16(spread_table()))
    vmem = pl.BlockSpec(memory_space=pltpu.VMEM)
    hbm = pl.BlockSpec(memory_space=pl.ANY)
    return pl.pallas_call(
        functools.partial(exchange_kernel, n_time, n_chan, per),
        in_specs=[vmem, vmem, hbm, hbm],
        out_specs=vmem,
        out_shape=jax.ShapeDtypeStruct((total, TILE), jnp.float32),
        scratch_shapes=[
            pltpu.VMEM((2, reach, n_chan, rows2, LANES), jnp.float32),
            pltpu.VMEM((n_chan, rows2, LANES), jnp.float32),
            pltpu.VMEM((n_chan, rows2, LANES), jnp.float32),
            pltpu.VMEM((n_time, 8, LANES), jnp.float32),
            pltpu.VMEM((n_time, 8, LANES), jnp.float32),
            pltpu.VMEM(delay.shape, jnp.bfloat16),
            pltpu.VMEM(spread.shape, jnp.bfloat16),
            pltpu.VMEM((8, TILE), jnp.float32),
            pltpu.SemaphoreType.DMA((2, reach, 2 * pieces)),
            pltpu.SemaphoreType.DMA((2, reach, 2 * pieces)),
            pltpu.SemaphoreType.DMA((n_chan,)),
            pltpu.SemaphoreType.DMA((n_chan,)),
            pltpu.SemaphoreType.DMA((n_time,)),
            pltpu.SemaphoreType.DMA((n_time,)),
            pltpu.SemaphoreType.DMA((2,)),
        ],
        compiler_params=pltpu.CompilerParams(collective_id=0, has_side_effects=True, vmem_limit_bytes=40 << 20),
        name="exchange",
    )(grid, wgrid, in_hbm(delay), in_hbm(spread))


def local(visibilities, vis_weight, tile_index, tile_offset, live_count):
    channels, parts, groups, slots = visibilities.shape
    n_chan = lax.axis_size("chan")
    n_time = lax.axis_size("tm")
    data = visibilities.reshape(channels * parts, groups, slots)
    grid, wgrid = gridding(data, vis_weight, tile_index, tile_offset, live_count, n_chan * n_time)
    result = exchange(grid, wgrid, n_time, n_chan)
    return result.reshape(2, channels * n_chan, TILE)


def solution(mesh):
    placed = (P("chan", None, "tm", None), P("tm", None), P("tm"), P("tm", None), P("tm", None))
    return jax.shard_map(
        local, mesh=mesh, in_specs=placed, out_specs=P(None, None, ("tm", "chan")), check_vma=False
    )
```

```python
import functools
import math

import jax
import jax.numpy as jnp
import ml_dtypes
import numpy as np
from jax import lax
from jax.experimental import pallas as pl
from jax.experimental.pallas import tpu as pltpu
from jax.sharding import PartitionSpec as P

TSIDE = 16
TILE = TSIDE * TSIDE
LANES = 128
KERNEL_SIGMA2 = 1.44
KERNEL_REACH = 3
HALVES = 2
MESH = pl.DeviceIdType.MESH


def split_bf16(table):
    high = table.astype(ml_dtypes.bfloat16)
    low = (table - high.astype(np.float64)).astype(ml_dtypes.bfloat16)
    return np.stack([high, low])


def spread_table():
    step = np.arange(TSIDE)[:, None] - np.arange(TSIDE)[None, :]
    line = np.where(np.abs(step) <= KERNEL_REACH, np.exp(-step * step / (2.0 * KERNEL_SIGMA2)), 0.0)
    return np.kron(line, line)


def delay_table(channels):
    freq = np.arange(channels)
    angle = 2.0 * np.pi * (freq[:, None] * freq[None, :] % channels) / channels
    phase = 2.0 * np.pi * freq / (channels - 1)
    taper = 0.42323 - 0.49755 * np.cos(phase) + 0.07922 * np.cos(2.0 * phase)
    cos_part = np.cos(angle) * taper[None, :]
    sin_part = np.sin(angle) * taper[None, :]
    upper = np.stack([cos_part, sin_part], axis=-1)
    lower = np.stack([-sin_part, cos_part], axis=-1)
    return np.stack([upper, lower], axis=0).reshape(2 * channels, 2 * channels)


def in_hbm(x):
    return pltpu.with_memory_space_constraint(x, pltpu.HBM)


BATCH = 16
PUSH = 4


def chunks_of(groups):
    cuts = [32, 96, 128]
    if groups < 2 * sum(cuts):
        return [groups]
    rest = groups - sum(cuts)
    return cuts + [rest // 2, rest - rest // 2]


def grid_kernel(
    live_hbm, tile_hbm, vis_hbm, weight_hbm, offset_hbm, grid_ref, wgrid_ref,
    live_ref, tile_ref, vis_ref, weight_ref, offset_ref, vis_sem, small_sem,
):
    rows, groups = vis_ref.shape[:2]
    cuts = chunks_of(groups)
    starts = [sum(cuts[:n]) for n in range(len(cuts))]

    def vis_copy(n):
        part = pl.ds(starts[n], cuts[n])
        return pltpu.make_async_copy(vis_hbm.at[:, part], vis_ref.at[:, part], vis_sem.at[n])

    pairs = [(weight_hbm, weight_ref), (offset_hbm, offset_ref), (live_hbm, live_ref), (tile_hbm, tile_ref)]
    small = [pltpu.make_async_copy(a, b, small_sem.at[n]) for n, (a, b) in enumerate(pairs)]
    vis_copy(0).start()
    for copy in small:
        copy.start()
    for n in range(1, len(cuts)):
        vis_copy(n).start()

    @pl.loop(0, grid_ref.shape[0] // 8)
    def _(i):
        some = pl.ds(i * 8, 8)
        grid_ref[some] = jnp.zeros((8, *grid_ref.shape[1:]), jnp.float32)
        wgrid_ref[some] = jnp.zeros((8, *wgrid_ref.shape[1:]), jnp.float32)

    for copy in small:
        copy.wait()

    cell = lax.broadcasted_iota(jnp.int32, (LANES, LANES), 0).astype(jnp.int16)
    lane = lax.broadcasted_iota(jnp.int32, (8, LANES), 1)
    sub = lax.broadcasted_iota(jnp.int32, (8, LANES), 0)
    zero = jnp.zeros((16, LANES), jnp.bfloat16)
    blank = jnp.zeros((HALVES * rows, LANES), jnp.bfloat16)

    def load(first):
        data = jnp.swapaxes(vis_ref[:, pl.ds(first, BATCH), :].astype(jnp.float32), 0, 1)
        return data, weight_ref[pl.ds(first, BATCH), :].astype(jnp.float32)

    def inner(*acc):
        sums, wsums = acc[:BATCH], acc[BATCH:]

        def feed(first, k, data, weights):
            hots, lefts, highs = [], [], []
            for i in range(PUSH):
                j = PUSH * k + i
                weight = jnp.where(lane < live_ref[0, first + j], jnp.broadcast_to(weights[j:j + 1], (8, LANES)), 0.0)
                offset = jnp.broadcast_to(offset_ref[pl.ds(first + j, 1), :], (8, LANES))
                low = jnp.bitwise_and(offset, LANES - 1)
                high = jnp.right_shift(offset, 7)
                low16 = jnp.concatenate([low, low], 0).astype(jnp.int16)
                weight16 = jnp.concatenate([weight, weight], 0).astype(jnp.bfloat16)
                hots.append(jnp.concatenate(
                    [jnp.where(cell[16 * q:16 * q + 16] == low16, weight16, zero) for q in range(LANES // 16)], 0
                ))
                highs.append(high)
                parts = [
                    jnp.where(high == a, data[j, 8 * q:8 * q + 8], 0.0) for a in range(HALVES) for q in range(rows // 8)
                ]
                left = jnp.concatenate(parts, 0).astype(jnp.bfloat16)
                lefts.append(jnp.concatenate([left, blank] if i % 2 == 0 else [blank, left], 1))
            ones = []
            for i in range(2):
                high = jnp.where(sub < 4, highs[i], highs[i + 2])
                mine = (jnp.bitwise_and(sub, 2) == 2 * i) & (high == jnp.bitwise_and(sub, 1))
                ones.append(jnp.where(mine, 1.0, 0.0))
            wleft = jnp.concatenate([jnp.concatenate(ones, 1), jnp.zeros((8, 2 * LANES), jnp.float32)], 0)
            turned = k >= BATCH // PUSH // 2
            if turned:
                hots = [hots[i].T for i in (0, 2, 1, 3)]
            right = jnp.concatenate([jnp.concatenate(hots[:2], 1), jnp.concatenate(hots[2:], 1)], 0)
            pltpu.matmul_push_rhs(right, k // 2, k % 2, transpose=not turned)
            for i in range(PUSH):
                pltpu.matmul_acc_lhs(sums[PUSH * k + i], lefts[i], load_staged_rhs=k // 2 if i == 0 else None)
            pltpu.matmul_acc_lhs(wsums[k], wleft.astype(jnp.bfloat16))

        def take(first, k):
            for i in range(PUSH):
                total = pltpu.matmul_pop(sums[PUSH * k + i])
                grid_ref[tile_ref[first + PUSH * k + i]] += total[:, :LANES] if i < 2 else total[:, LANES:]
            total = pltpu.matmul_pop(wsums[k])
            for i in range(PUSH):
                own = total[:8, :LANES] if i < 2 else total[:8, LANES:]
                wgrid_ref[tile_ref[first + PUSH * k + i]] += jnp.where(jnp.right_shift(sub, 1) == i, own, 0.0)

        def body(index, _):
            first = pl.multiple_of(index * BATCH, BATCH)
            data, weights = load(first)
            for k in range(BATCH // PUSH):
                take(first - BATCH, k)
                feed(first, k, data, weights)
            return 0

        vis_copy(0).wait()
        data, weights = load(0)
        for k in range(BATCH // PUSH):
            feed(0, k, data, weights)
        for n in range(len(cuts)):
            if n > 0:
                vis_copy(n).wait()
            low, high = max(1, starts[n] // BATCH), (starts[n] + cuts[n]) // BATCH
            lax.fori_loop(low, high, body, 0, unroll=next((u for u in (8, 4, 3, 2) if (high - low) % u == 0 and high - low > u), 1))
        for k in range(BATCH // PUSH):
            take(groups - BATCH, k)

    def space(unit, depth):
        return pltpu.ACC(unit)((depth, 2 * LANES), jnp.float32)

    pl.run_scoped(
        inner,
        *[space(k % 2, HALVES * rows) for k in range(BATCH // PUSH) for i in range(PUSH)],
        *[space(k % 2, 16) for k in range(BATCH // PUSH)],
    )


def gridding(data, weight, tiles, offset, live, n_tile):
    rows, groups, slots = data.shape
    hbm = pl.BlockSpec(memory_space=pltpu.HBM)
    vmem = pl.BlockSpec(memory_space=pltpu.VMEM)
    return pl.pallas_call(
        grid_kernel,
        in_specs=[hbm] * 5,
        out_specs=[vmem, vmem],
        out_shape=[
            jax.ShapeDtypeStruct((n_tile, HALVES * rows, LANES), jnp.float32),
            jax.ShapeDtypeStruct((n_tile, 8, LANES), jnp.float32),
        ],
        scratch_shapes=[
            pltpu.SMEM(live.shape, jnp.int32),
            pltpu.SMEM(tiles.shape, jnp.int32),
            pltpu.VMEM(data.shape, data.dtype),
            pltpu.VMEM(weight.shape, weight.dtype),
            pltpu.VMEM(offset.shape, jnp.int32),
            pltpu.SemaphoreType.DMA((len(chunks_of(groups)),)),
            pltpu.SemaphoreType.DMA((4,)),
        ],
        compiler_params=pltpu.CompilerParams(vmem_limit_bytes=24 << 20),
        cost_estimate=pl.CostEstimate(flops=2 * groups * rows * slots * TILE, bytes_accessed=data.size * 2, transcendentals=0),
        name="gridding",
    )(*[in_hbm(x) for x in (live, tiles, data, weight, offset)])


def dot3(left, right):
    dot = functools.partial(jnp.dot, preferred_element_type=jnp.float32)
    return dot(left[0], right[0]) + (dot(left[0], right[1]) + dot(left[1], right[0]))


def pair(x):
    high = x.astype(jnp.bfloat16)
    return high, (x - high.astype(jnp.float32)).astype(jnp.bfloat16)


def exchange_kernel(
    n_time, n_chan, per, grid_ref, wgrid_ref, delay_hbm, spread_hbm, out_ref,
    ring, mine, gathered, wown, wparts, delay, spread, scale,
    ring_send, ring_recv, plane_send, plane_recv, w_send, w_recv, table_sem,
):
    me_t = lax.axis_index("tm")
    me_c = lax.axis_index("chan")
    pieces = n_chan // per
    wide = pieces // 2
    reach = n_time // 2
    last = reach - 1
    fine = 2 if per % 2 == 0 else 1
    rows2 = grid_ref.shape[1]
    rows = rows2 // HALVES
    turn = me_c // per
    neighbour = (lax.rem(me_t + 1, n_time), lax.rem(me_t + n_time - 1, n_time))

    tables = [pltpu.make_async_copy(delay_hbm, delay, table_sem.at[0]),
              pltpu.make_async_copy(spread_hbm, spread, table_sem.at[1])]
    for copy in tables:
        copy.start()

    barrier = pltpu.get_barrier_semaphore()

    def greet_t(k, _):
        pl.semaphore_signal(barrier, inc=1, device_id={"tm": lax.rem(me_t + k, n_time)}, device_id_type=MESH)
        return 0

    def greet_c(k, _):
        pl.semaphore_signal(barrier, inc=1, device_id={"chan": lax.rem(me_c + k, n_chan)}, device_id_type=MESH)
        return 0

    greet_t(1, 0)
    greet_t(n_time - 1, 0)
    lax.fori_loop(2, n_time - 1, greet_t, 0)
    lax.fori_loop(1, n_chan, greet_c, 0)

    pl.semaphore_wait(barrier, n_time - 1 + n_chan - 1)

    def away(slot):
        if wide != 4:
            return lax.rem(slot + 1, wide)
        late = slot // 2
        return (2 + slot) * (1 - late) + (3 - slot) * late

    def pair_of(slot):
        return lax.rem(away(slot) + turn // 2, wide)

    def piece_of(slot):
        return 2 * pair_of(slot // 2) + lax.rem(slot + turn + 1, 2)

    def span(step, slot):
        if step < last:
            return pl.ds(pair_of(slot) * (2 * per), 2 * per)
        return pl.ds(piece_of(slot // fine) * per + lax.rem(slot, fine) * (per // fine), per // fine)

    def grid_span(chunk, step, slot):
        if step < last:
            return pl.ds(chunk * n_chan + pair_of(slot) * (2 * per), 2 * per)
        return pl.ds(chunk * n_chan + piece_of(slot // fine) * per + lax.rem(slot, fine) * (per // fine), per // fine)

    def chunk_of(way, step):
        hops = reach - step
        return lax.rem(me_t + (hops if way == 0 else n_time - hops), n_time)

    def ring_copy(way, step, slot, raw):
        where = span(step, slot)
        source = grid_ref.at[grid_span(chunk_of(way, step), step, slot)] if raw else ring.at[way, step - 1, where]
        return pltpu.make_async_remote_copy(
            src_ref=source,
            dst_ref=ring.at[way, step, where],
            send_sem=ring_send.at[way, step, slot],
            recv_sem=ring_recv.at[way, step, slot],
            device_id={"tm": neighbour[way]},
            device_id_type=MESH,
        )

    half = wide // 2

    def open_ring(slot, _):
        ring_copy(0, 0, slot, True).start()
        ring_copy(1, 0, slot + half, True).start()
        return 0

    lax.fori_loop(0, half, open_ring, 0)

    for t in range(n_time):
        part = wgrid_ref[t * n_chan + me_c]
        total = part[0:HALVES]
        for i in range(1, PUSH):
            total = total + part[HALVES * i:HALVES * (i + 1)]
        wown[t, 0:HALVES] = total

    def w_copy(k):
        other = lax.rem(me_t + k, n_time)
        return pltpu.make_async_remote_copy(
            src_ref=wown.at[other, pl.ds(0, HALVES)],
            dst_ref=wparts.at[k, pl.ds(0, HALVES)],
            send_sem=w_send.at[k],
            recv_sem=w_recv.at[k],
            device_id={"tm": other},
            device_id_type=MESH,
        )

    lax.fori_loop(1, n_time, lambda k, _: (w_copy(k).start(), 0)[1], 0)

    def hop(step, fresh):
        def body(slot, _):
            for way in range(2):
                if not fresh[way]:
                    ring_copy(way, step - 1, slot, True).wait_recv()
                    ring[way, step - 1, span(step - 1, slot)] += grid_ref[grid_span(chunk_of(way, step), step - 1, slot)]
                if step < last:
                    ring_copy(way, step, slot, fresh[way]).start()
            if step == last:
                for q in range(2 * fine):
                    for way in range(2):
                        ring_copy(way, step, 2 * fine * slot + q, fresh[way]).start()
            return 0
        return body

    lax.fori_loop(0, half, hop(1, (False, True)), 0)
    lax.fori_loop(half, wide, hop(1, (True, False)), 0)
    for step in range(2, reach):
        lax.fori_loop(0, wide, hop(step, (False, False)), 0)

    def plane_copy(other):
        return pltpu.make_async_remote_copy(
            src_ref=mine.at[other],
            dst_ref=gathered.at[me_c],
            send_sem=plane_send.at[other],
            recv_sem=plane_recv.at[me_c],
            device_id={"chan": other},
            device_id_type=MESH,
        )

    lax.fori_loop(1, n_time, lambda k, _: (w_copy(k).wait_recv(), 0)[1], 0)
    wsum = wown[me_t, 0:HALVES]
    for k in range(1, n_time):
        wsum = wsum + wparts[k, 0:HALVES]
    for copy in tables:
        copy.wait()
    wcells = jnp.concatenate([jnp.broadcast_to(wsum[a:a + 1], (8, LANES)) for a in range(HALVES)], 1)
    spread_pair = (spread[0], spread[1])
    scale[...] = jnp.broadcast_to(1.0 / jnp.maximum(dot3(pair(wcells), spread_pair), 1.0), scale.shape)

    def finish(slot, _):
        for way in range(2):
            ring_copy(way, last, slot, True).wait_recv()
        where = span(last, slot)
        mine[where] = grid_ref[grid_span(me_t, last, slot)] + ring[0, last, where] + ring[1, last, where]
        for q in range(per // fine):
            other = piece_of(slot // fine) * per + lax.rem(slot, fine) * (per // fine) + q

            @pl.when(other != me_c)
            def _():
                plane_copy(other).start()

            @pl.when(other == me_c)
            def _():
                gathered[me_c] = mine[me_c]
        return 0

    def absorb(slot, first):
        block = 2 * lax.rem(turn // 2 + wide - away(slot // 2), wide) + lax.rem(turn + pieces - slot - 1, 2)
        for q in range(per):
            other = block * per + q

            @pl.when(other != me_c)
            def _():
                pltpu.make_async_remote_copy(
                    src_ref=mine.at[other],
                    dst_ref=gathered.at[other],
                    send_sem=plane_send.at[other],
                    recv_sem=plane_recv.at[other],
                    device_id={"chan": other},
                    device_id_type=MESH,
                ).wait_recv()

        some = gathered[pl.ds(block * per, per)]
        cells = jnp.concatenate([some[:, a * rows:(a + 1) * rows, :].reshape(per * rows, LANES) for a in range(HALVES)], 1)
        normal = dot3(pair(cells), spread_pair) * scale[0:1]
        high, low = pair(normal)
        part = jnp.dot(delay[block], jnp.concatenate([high, high, low], 0), preferred_element_type=jnp.float32)
        out_ref[...] = part if first else out_ref[...] + part

    lag = min(3, pieces - 1)

    def whole(slot):
        for f in range(fine):
            finish(slot * fine + f, 0)

    def both(slot, _):
        absorb(slot - lag, False)
        whole(slot)
        return 0

    def drain_ring(way, step, low, high):
        lax.fori_loop(low, high, lambda slot, _: (ring_copy(way, step, slot, True).wait_send(), 0)[1], 0)

    drain_ring(0, 0, 0, half)
    drain_ring(1, 0, half, wide)
    for step in range(1, last):
        for way in range(2):
            drain_ring(way, step, 0, wide)
    lax.fori_loop(1, n_time, lambda k, _: (w_copy(k).wait_send(), 0)[1], 0)

    for slot in range(lag):
        whole(slot)
    absorb(0, True)
    whole(lag)
    lax.fori_loop(lag + 1, pieces, both, 0)
    for way in range(2):
        drain_ring(way, last, 0, pieces * fine)
    lax.fori_loop(pieces - lag, pieces - 1, lambda k, _: (absorb(k, False), 0)[1], 0)
    lax.fori_loop(1, n_chan, lambda k, _: (plane_copy(lax.rem(me_c + k, n_chan)).wait_send(), 0)[1], 0)
    absorb(pieces - 1, False)


def exchange(grid, wgrid, n_time, n_chan):
    rows2 = grid.shape[1]
    rows = rows2 // HALVES
    total = rows * n_chan
    per = max(1, n_chan // 8)
    pieces = n_chan // per
    reach = n_time // 2
    table = split_bf16(delay_table(total // 2)).reshape(2, total, pieces, per * rows)
    delay = jnp.asarray(np.concatenate([table[0], table[1], table[0]], -1).transpose(1, 0, 2))
    spread = jnp.asarray(split_bf16(spread_table()))
    vmem = pl.BlockSpec(memory_space=pltpu.VMEM)
    hbm = pl.BlockSpec(memory_space=pl.ANY)
    return pl.pallas_call(
        functools.partial(exchange_kernel, n_time, n_chan, per),
        in_specs=[vmem, vmem, hbm, hbm],
        out_specs=vmem,
        out_shape=jax.ShapeDtypeStruct((total, TILE), jnp.float32),
        scratch_shapes=[
            pltpu.VMEM((2, reach, n_chan, rows2, LANES), jnp.float32),
            pltpu.VMEM((n_chan, rows2, LANES), jnp.float32),
            pltpu.VMEM((n_chan, rows2, LANES), jnp.float32),
            pltpu.VMEM((n_time, 8, LANES), jnp.float32),
            pltpu.VMEM((n_time, 8, LANES), jnp.float32),
            pltpu.VMEM(delay.shape, jnp.bfloat16),
            pltpu.VMEM(spread.shape, jnp.bfloat16),
            pltpu.VMEM((8, TILE), jnp.float32),
            pltpu.SemaphoreType.DMA((2, reach, 2 * pieces)),
            pltpu.SemaphoreType.DMA((2, reach, 2 * pieces)),
            pltpu.SemaphoreType.DMA((n_chan,)),
            pltpu.SemaphoreType.DMA((n_chan,)),
            pltpu.SemaphoreType.DMA((n_time,)),
            pltpu.SemaphoreType.DMA((n_time,)),
            pltpu.SemaphoreType.DMA((2,)),
        ],
        compiler_params=pltpu.CompilerParams(collective_id=0, has_side_effects=True, vmem_limit_bytes=40 << 20),
        name="exchange",
    )(grid, wgrid, in_hbm(delay), in_hbm(spread))


def local(visibilities, vis_weight, tile_index, tile_offset, live_count):
    channels, parts, groups, slots = visibilities.shape
    n_chan = lax.axis_size("chan")
    n_time = lax.axis_size("tm")
    data = visibilities.reshape(channels * parts, groups, slots)
    grid, wgrid = gridding(data, vis_weight, tile_index, tile_offset, live_count, n_chan * n_time)
    result = exchange(grid, wgrid, n_time, n_chan)
    return result.reshape(2, channels * n_chan, TILE)


def solution(mesh):
    placed = (P("chan", None, "tm", None), P("tm", None), P("tm"), P("tm", None), P("tm", None))
    return jax.shard_map(
        local, mesh=mesh, in_specs=placed, out_specs=P(None, None, ("tm", "chan")), check_vma=False
    )
```

```python
import functools
import math

import jax
import jax.numpy as jnp
import ml_dtypes
import numpy as np
from jax import lax
from jax.experimental import pallas as pl
from jax.experimental.pallas import tpu as pltpu
from jax.sharding import PartitionSpec as P

TSIDE = 16
TILE = TSIDE * TSIDE
LANES = 128
KERNEL_SIGMA2 = 1.44
KERNEL_REACH = 3
HALVES = 2
MESH = pl.DeviceIdType.MESH


def split_bf16(table):
    high = table.astype(ml_dtypes.bfloat16)
    low = (table - high.astype(np.float64)).astype(ml_dtypes.bfloat16)
    return np.stack([high, low])


def spread_table():
    step = np.arange(TSIDE)[:, None] - np.arange(TSIDE)[None, :]
    line = np.where(np.abs(step) <= KERNEL_REACH, np.exp(-step * step / (2.0 * KERNEL_SIGMA2)), 0.0)
    return np.kron(line, line)


def delay_table(channels):
    freq = np.arange(channels)
    angle = 2.0 * np.pi * (freq[:, None] * freq[None, :] % channels) / channels
    phase = 2.0 * np.pi * freq / (channels - 1)
    taper = 0.42323 - 0.49755 * np.cos(phase) + 0.07922 * np.cos(2.0 * phase)
    cos_part = np.cos(angle) * taper[None, :]
    sin_part = np.sin(angle) * taper[None, :]
    upper = np.stack([cos_part, sin_part], axis=-1)
    lower = np.stack([-sin_part, cos_part], axis=-1)
    return np.stack([upper, lower], axis=0).reshape(2 * channels, 2 * channels)


def in_hbm(x):
    return pltpu.with_memory_space_constraint(x, pltpu.HBM)


BATCH = 16
PUSH = 4


def chunks_of(groups):
    cuts = [32, 96, 128]
    if groups < 2 * sum(cuts):
        return [groups]
    return cuts + [groups - sum(cuts)]


def grid_kernel(
    live_hbm, tile_hbm, vis_hbm, weight_hbm, offset_hbm, grid_ref, wgrid_ref,
    live_ref, tile_ref, vis_ref, weight_ref, offset_ref, vis_sem, small_sem,
):
    rows, groups = vis_ref.shape[:2]
    cuts = chunks_of(groups)
    starts = [sum(cuts[:n]) for n in range(len(cuts))]

    def vis_copy(n):
        part = pl.ds(starts[n], cuts[n])
        return pltpu.make_async_copy(vis_hbm.at[:, part], vis_ref.at[:, part], vis_sem.at[n])

    pairs = [(weight_hbm, weight_ref), (offset_hbm, offset_ref), (live_hbm, live_ref), (tile_hbm, tile_ref)]
    small = [pltpu.make_async_copy(a, b, small_sem.at[n]) for n, (a, b) in enumerate(pairs)]
    vis_copy(0).start()
    for copy in small:
        copy.start()
    for n in range(1, len(cuts)):
        vis_copy(n).start()

    @pl.loop(0, grid_ref.shape[0] // 8)
    def _(i):
        some = pl.ds(i * 8, 8)
        grid_ref[some] = jnp.zeros((8, *grid_ref.shape[1:]), jnp.float32)
        wgrid_ref[some] = jnp.zeros((8, *wgrid_ref.shape[1:]), jnp.float32)

    for copy in small:
        copy.wait()

    cell = lax.broadcasted_iota(jnp.int32, (LANES, LANES), 0).astype(jnp.int16)
    lane = lax.broadcasted_iota(jnp.int32, (8, LANES), 1)
    sub = lax.broadcasted_iota(jnp.int32, (8, LANES), 0)
    zero = jnp.zeros((16, LANES), jnp.bfloat16)
    blank = jnp.zeros((HALVES * rows, LANES), jnp.bfloat16)

    def load(first):
        data = jnp.swapaxes(vis_ref[:, pl.ds(first, BATCH), :].astype(jnp.float32), 0, 1)
        return data, weight_ref[pl.ds(first, BATCH), :].astype(jnp.float32)

    def inner(*acc):
        sums, wsums = acc[:BATCH], acc[BATCH:]

        def feed(first, k, data, weights):
            hots, lefts, highs = [], [], []
            for i in range(PUSH):
                j = PUSH * k + i
                weight = jnp.where(lane < live_ref[0, first + j], jnp.broadcast_to(weights[j:j + 1], (8, LANES)), 0.0)
                offset = jnp.broadcast_to(offset_ref[pl.ds(first + j, 1), :], (8, LANES))
                low = jnp.bitwise_and(offset, LANES - 1)
                high = jnp.right_shift(offset, 7)
                low16 = jnp.concatenate([low, low], 0).astype(jnp.int16)
                weight16 = jnp.concatenate([weight, weight], 0).astype(jnp.bfloat16)
                hots.append(jnp.concatenate(
                    [jnp.where(cell[16 * q:16 * q + 16] == low16, weight16, zero) for q in range(LANES // 16)], 0
                ))
                highs.append(high)
                parts = [
                    jnp.where(high == a, data[j, 8 * q:8 * q + 8], 0.0) for a in range(HALVES) for q in range(rows // 8)
                ]
                left = jnp.concatenate(parts, 0).astype(jnp.bfloat16)
                lefts.append(jnp.concatenate([left, blank] if i % 2 == 0 else [blank, left], 1))
            ones = []
            for i in range(2):
                high = jnp.where(sub < 4, highs[i], highs[i + 2])
                mine = (jnp.bitwise_and(sub, 2) == 2 * i) & (high == jnp.bitwise_and(sub, 1))
                ones.append(jnp.where(mine, 1.0, 0.0))
            wleft = jnp.concatenate([jnp.concatenate(ones, 1), jnp.zeros((8, 2 * LANES), jnp.float32)], 0)
            turned = k >= BATCH // PUSH // 2
            if turned:
                hots = [hots[i].T for i in (0, 2, 1, 3)]
            right = jnp.concatenate([jnp.concatenate(hots[:2], 1), jnp.concatenate(hots[2:], 1)], 0)
            pltpu.matmul_push_rhs(right, k // 2, k % 2, transpose=not turned)
            for i in range(PUSH):
                pltpu.matmul_acc_lhs(sums[PUSH * k + i], lefts[i], load_staged_rhs=k // 2 if i == 0 else None)
            pltpu.matmul_acc_lhs(wsums[k], wleft.astype(jnp.bfloat16))

        def take(first, k):
            for i in range(PUSH):
                total = pltpu.matmul_pop(sums[PUSH * k + i])
                grid_ref[tile_ref[first + PUSH * k + i]] += total[:, :LANES] if i < 2 else total[:, LANES:]
            total = pltpu.matmul_pop(wsums[k])
            for i in range(PUSH):
                own = total[:8, :LANES] if i < 2 else total[:8, LANES:]
                wgrid_ref[tile_ref[first + PUSH * k + i]] += jnp.where(jnp.right_shift(sub, 1) == i, own, 0.0)

        def body(index, _):
            first = pl.multiple_of(index * BATCH, BATCH)
            data, weights = load(first)
            for k in range(BATCH // PUSH):
                take(first - BATCH, k)
                feed(first, k, data, weights)
            return 0

        vis_copy(0).wait()
        data, weights = load(0)
        for k in range(BATCH // PUSH):
            feed(0, k, data, weights)
        for n in range(len(cuts)):
            if n > 0:
                vis_copy(n).wait()
            low, high = max(1, starts[n] // BATCH), (starts[n] + cuts[n]) // BATCH
            lax.fori_loop(low, high, body, 0, unroll=next((u for u in (16, 8, 4, 3, 2) if (high - low) % u == 0 and high - low > u), 1))
        for k in range(BATCH // PUSH):
            take(groups - BATCH, k)

    def space(unit, depth):
        return pltpu.ACC(unit)((depth, 2 * LANES), jnp.float32)

    pl.run_scoped(
        inner,
        *[space(k % 2, HALVES * rows) for k in range(BATCH // PUSH) for i in range(PUSH)],
        *[space(k % 2, 16) for k in range(BATCH // PUSH)],
    )


def gridding(data, weight, tiles, offset, live, n_tile):
    rows, groups, slots = data.shape
    hbm = pl.BlockSpec(memory_space=pltpu.HBM)
    vmem = pl.BlockSpec(memory_space=pltpu.VMEM)
    return pl.pallas_call(
        grid_kernel,
        in_specs=[hbm] * 5,
        out_specs=[vmem, vmem],
        out_shape=[
            jax.ShapeDtypeStruct((n_tile, HALVES * rows, LANES), jnp.float32),
            jax.ShapeDtypeStruct((n_tile, 8, LANES), jnp.float32),
        ],
        scratch_shapes=[
            pltpu.SMEM(live.shape, jnp.int32),
            pltpu.SMEM(tiles.shape, jnp.int32),
            pltpu.VMEM(data.shape, data.dtype),
            pltpu.VMEM(weight.shape, weight.dtype),
            pltpu.VMEM(offset.shape, jnp.int32),
            pltpu.SemaphoreType.DMA((len(chunks_of(groups)),)),
            pltpu.SemaphoreType.DMA((4,)),
        ],
        compiler_params=pltpu.CompilerParams(vmem_limit_bytes=24 << 20),
        cost_estimate=pl.CostEstimate(flops=2 * groups * rows * slots * TILE, bytes_accessed=data.size * 2, transcendentals=0),
        name="gridding",
    )(*[in_hbm(x) for x in (live, tiles, data, weight, offset)])


def dot3(left, right):
    dot = functools.partial(jnp.dot, preferred_element_type=jnp.float32)
    return dot(left[0], right[0]) + (dot(left[0], right[1]) + dot(left[1], right[0]))


def pair(x):
    high = x.astype(jnp.bfloat16)
    return high, (x - high.astype(jnp.float32)).astype(jnp.bfloat16)


def exchange_kernel(
    n_time, n_chan, per, grid_ref, wgrid_ref, delay_hbm, spread_hbm, out_ref,
    ring, mine, gathered, wown, wparts, delay, spread, scale,
    ring_send, ring_recv, plane_send, plane_recv, w_send, w_recv, table_sem,
):
    me_t = lax.axis_index("tm")
    me_c = lax.axis_index("chan")
    pieces = n_chan // per
    wide = pieces // 2
    reach = n_time // 2
    last = reach - 1
    fine = 2 if per % 2 == 0 else 1
    rows2 = grid_ref.shape[1]
    rows = rows2 // HALVES
    turn = me_c // per
    neighbour = (lax.rem(me_t + 1, n_time), lax.rem(me_t + n_time - 1, n_time))

    tables = [pltpu.make_async_copy(delay_hbm, delay, table_sem.at[0]),
              pltpu.make_async_copy(spread_hbm, spread, table_sem.at[1])]
    for copy in tables:
        copy.start()

    barrier = pltpu.get_barrier_semaphore()

    def greet_t(k, _):
        pl.semaphore_signal(barrier, inc=1, device_id={"tm": lax.rem(me_t + k, n_time)}, device_id_type=MESH)
        return 0

    def greet_c(k, _):
        pl.semaphore_signal(barrier, inc=1, device_id={"chan": lax.rem(me_c + k, n_chan)}, device_id_type=MESH)
        return 0

    greet_t(1, 0)
    greet_t(n_time - 1, 0)
    lax.fori_loop(2, n_time - 1, greet_t, 0)
    lax.fori_loop(1, n_chan, greet_c, 0)

    pl.semaphore_wait(barrier, n_time - 1 + n_chan - 1)

    def away(slot):
        if wide != 4:
            return lax.rem(slot + 1, wide)
        late = slot // 2
        return (2 + slot) * (1 - late) + (3 - slot) * late

    def pair_of(slot):
        return lax.rem(away(slot) + turn // 2, wide)

    def piece_of(slot):
        return 2 * pair_of(slot // 2) + lax.rem(slot + turn + 1, 2)

    def span(step, slot):
        if step < last:
            return pl.ds(pair_of(slot) * (2 * per), 2 * per)
        return pl.ds(piece_of(slot // fine) * per + lax.rem(slot, fine) * (per // fine), per // fine)

    def grid_span(chunk, step, slot):
        if step < last:
            return pl.ds(chunk * n_chan + pair_of(slot) * (2 * per), 2 * per)
        return pl.ds(chunk * n_chan + piece_of(slot // fine) * per + lax.rem(slot, fine) * (per // fine), per // fine)

    def chunk_of(way, step):
        hops = reach - step
        return lax.rem(me_t + (hops if way == 0 else n_time - hops), n_time)

    def ring_copy(way, step, slot, raw):
        where = span(step, slot)
        source = grid_ref.at[grid_span(chunk_of(way, step), step, slot)] if raw else ring.at[way, step - 1, where]
        return pltpu.make_async_remote_copy(
            src_ref=source,
            dst_ref=ring.at[way, step, where],
            send_sem=ring_send.at[way, step, slot],
            recv_sem=ring_recv.at[way, step, slot],
            device_id={"tm": neighbour[way]},
            device_id_type=MESH,
        )

    half = wide // 2

    def open_ring(slot, _):
        ring_copy(0, 0, slot, True).start()
        ring_copy(1, 0, slot + half, True).start()
        return 0

    lax.fori_loop(0, half, open_ring, 0)

    for t in range(n_time):
        part = wgrid_ref[t * n_chan + me_c]
        total = part[0:HALVES]
        for i in range(1, PUSH):
            total = total + part[HALVES * i:HALVES * (i + 1)]
        wown[t, 0:HALVES] = total

    def w_copy(k):
        other = lax.rem(me_t + k, n_time)
        return pltpu.make_async_remote_copy(
            src_ref=wown.at[other, pl.ds(0, HALVES)],
            dst_ref=wparts.at[k, pl.ds(0, HALVES)],
            send_sem=w_send.at[k],
            recv_sem=w_recv.at[k],
            device_id={"tm": other},
            device_id_type=MESH,
        )

    lax.fori_loop(1, n_time, lambda k, _: (w_copy(k).start(), 0)[1], 0)

    def hop(step, fresh):
        def body(slot, _):
            for way in range(2):
                if not fresh[way]:
                    ring_copy(way, step - 1, slot, True).wait_recv()
                    ring[way, step - 1, span(step - 1, slot)] += grid_ref[grid_span(chunk_of(way, step), step - 1, slot)]
                if step < last:
                    ring_copy(way, step, slot, fresh[way]).start()
            if step == last:
                for q in range(2 * fine):
                    for way in range(2):
                        ring_copy(way, step, 2 * fine * slot + q, fresh[way]).start()
            return 0
        return body

    lax.fori_loop(0, half, hop(1, (False, True)), 0)
    lax.fori_loop(half, wide, hop(1, (True, False)), 0)
    for step in range(2, reach):
        lax.fori_loop(0, wide, hop(step, (False, False)), 0)

    def plane_copy(other):
        return pltpu.make_async_remote_copy(
            src_ref=mine.at[other],
            dst_ref=gathered.at[me_c],
            send_sem=plane_send.at[other],
            recv_sem=plane_recv.at[me_c],
            device_id={"chan": other},
            device_id_type=MESH,
        )

    lax.fori_loop(1, n_time, lambda k, _: (w_copy(k).wait_recv(), 0)[1], 0)
    wsum = wown[me_t, 0:HALVES]
    for k in range(1, n_time):
        wsum = wsum + wparts[k, 0:HALVES]
    for copy in tables:
        copy.wait()
    wcells = jnp.concatenate([jnp.broadcast_to(wsum[a:a + 1], (8, LANES)) for a in range(HALVES)], 1)
    spread_pair = (spread[0], spread[1])
    scale[...] = jnp.broadcast_to(1.0 / jnp.maximum(dot3(pair(wcells), spread_pair), 1.0), scale.shape)

    def finish(slot, _):
        for way in range(2):
            ring_copy(way, last, slot, True).wait_recv()
        where = span(last, slot)
        mine[where] = grid_ref[grid_span(me_t, last, slot)] + ring[0, last, where] + ring[1, last, where]
        for q in range(per // fine):
            other = piece_of(slot // fine) * per + lax.rem(slot, fine) * (per // fine) + q

            @pl.when(other != me_c)
            def _():
                plane_copy(other).start()

            @pl.when(other == me_c)
            def _():
                gathered[me_c] = mine[me_c]
        return 0

    def absorb(slot, first):
        block = 2 * lax.rem(turn // 2 + wide - away(slot // 2), wide) + lax.rem(turn + pieces - slot - 1, 2)
        for q in range(per):
            other = block * per + q

            @pl.when(other != me_c)
            def _():
                pltpu.make_async_remote_copy(
                    src_ref=mine.at[other],
                    dst_ref=gathered.at[other],
                    send_sem=plane_send.at[other],
                    recv_sem=plane_recv.at[other],
                    device_id={"chan": other},
                    device_id_type=MESH,
                ).wait_recv()

        some = gathered[pl.ds(block * per, per)]
        cells = jnp.concatenate([some[:, a * rows:(a + 1) * rows, :].reshape(per * rows, LANES) for a in range(HALVES)], 1)
        normal = dot3(pair(cells), spread_pair) * scale[0:1]
        high, low = pair(normal)
        part = jnp.dot(delay[block], jnp.concatenate([high, high, low], 0), preferred_element_type=jnp.float32)
        out_ref[...] = part if first else out_ref[...] + part

    lag = min(3, pieces - 1)

    def whole(slot):
        for f in range(fine):
            finish(slot * fine + f, 0)

    def both(slot, _):
        absorb(slot - lag, False)
        whole(slot)
        return 0

    def drain_ring(way, step, low, high):
        lax.fori_loop(low, high, lambda slot, _: (ring_copy(way, step, slot, True).wait_send(), 0)[1], 0)

    drain_ring(0, 0, 0, half)
    drain_ring(1, 0, half, wide)
    for step in range(1, last):
        for way in range(2):
            drain_ring(way, step, 0, wide)
    lax.fori_loop(1, n_time, lambda k, _: (w_copy(k).wait_send(), 0)[1], 0)

    for slot in range(lag):
        whole(slot)
    absorb(0, True)
    whole(lag)
    lax.fori_loop(lag + 1, pieces, both, 0)
    for way in range(2):
        drain_ring(way, last, 0, pieces * fine)
    lax.fori_loop(pieces - lag, pieces - 1, lambda k, _: (absorb(k, False), 0)[1], 0)
    lax.fori_loop(1, n_chan, lambda k, _: (plane_copy(lax.rem(me_c + k, n_chan)).wait_send(), 0)[1], 0)
    absorb(pieces - 1, False)


def exchange(grid, wgrid, n_time, n_chan):
    rows2 = grid.shape[1]
    rows = rows2 // HALVES
    total = rows * n_chan
    per = max(1, n_chan // 8)
    pieces = n_chan // per
    reach = n_time // 2
    table = split_bf16(delay_table(total // 2)).reshape(2, total, pieces, per * rows)
    delay = jnp.asarray(np.concatenate([table[0], table[1], table[0]], -1).transpose(1, 0, 2))
    spread = jnp.asarray(split_bf16(spread_table()))
    vmem = pl.BlockSpec(memory_space=pltpu.VMEM)
    hbm = pl.BlockSpec(memory_space=pl.ANY)
    return pl.pallas_call(
        functools.partial(exchange_kernel, n_time, n_chan, per),
        in_specs=[vmem, vmem, hbm, hbm],
        out_specs=vmem,
        out_shape=jax.ShapeDtypeStruct((total, TILE), jnp.float32),
        scratch_shapes=[
            pltpu.VMEM((2, reach, n_chan, rows2, LANES), jnp.float32),
            pltpu.VMEM((n_chan, rows2, LANES), jnp.float32),
            pltpu.VMEM((n_chan, rows2, LANES), jnp.float32),
            pltpu.VMEM((n_time, 8, LANES), jnp.float32),
            pltpu.VMEM((n_time, 8, LANES), jnp.float32),
            pltpu.VMEM(delay.shape, jnp.bfloat16),
            pltpu.VMEM(spread.shape, jnp.bfloat16),
            pltpu.VMEM((8, TILE), jnp.float32),
            pltpu.SemaphoreType.DMA((2, reach, 2 * pieces)),
            pltpu.SemaphoreType.DMA((2, reach, 2 * pieces)),
            pltpu.SemaphoreType.DMA((n_chan,)),
            pltpu.SemaphoreType.DMA((n_chan,)),
            pltpu.SemaphoreType.DMA((n_time,)),
            pltpu.SemaphoreType.DMA((n_time,)),
            pltpu.SemaphoreType.DMA((2,)),
        ],
        compiler_params=pltpu.CompilerParams(collective_id=0, has_side_effects=True, vmem_limit_bytes=40 << 20),
        name="exchange",
    )(grid, wgrid, in_hbm(delay), in_hbm(spread))


def local(visibilities, vis_weight, tile_index, tile_offset, live_count):
    channels, parts, groups, slots = visibilities.shape
    n_chan = lax.axis_size("chan")
    n_time = lax.axis_size("tm")
    data = visibilities.reshape(channels * parts, groups, slots)
    grid, wgrid = gridding(data, vis_weight, tile_index, tile_offset, live_count, n_chan * n_time)
    result = exchange(grid, wgrid, n_time, n_chan)
    return result.reshape(2, channels * n_chan, TILE)


def solution(mesh):
    placed = (P("chan", None, "tm", None), P("tm", None), P("tm"), P("tm", None), P("tm", None))
    return jax.shard_map(
        local, mesh=mesh, in_specs=placed, out_specs=P(None, None, ("tm", "chan")), check_vma=False
    )
```

```python
import functools
import math

import jax
import jax.numpy as jnp
import ml_dtypes
import numpy as np
from jax import lax
from jax.experimental import pallas as pl
from jax.experimental.pallas import tpu as pltpu
from jax.sharding import PartitionSpec as P

TSIDE = 16
TILE = TSIDE * TSIDE
LANES = 128
KERNEL_SIGMA2 = 1.44
KERNEL_REACH = 3
HALVES = 2
MESH = pl.DeviceIdType.MESH


def split_bf16(table):
    high = table.astype(ml_dtypes.bfloat16)
    low = (table - high.astype(np.float64)).astype(ml_dtypes.bfloat16)
    return np.stack([high, low])


def spread_table():
    step = np.arange(TSIDE)[:, None] - np.arange(TSIDE)[None, :]
    line = np.where(np.abs(step) <= KERNEL_REACH, np.exp(-step * step / (2.0 * KERNEL_SIGMA2)), 0.0)
    return np.kron(line, line)


def delay_table(channels):
    freq = np.arange(channels)
    angle = 2.0 * np.pi * (freq[:, None] * freq[None, :] % channels) / channels
    phase = 2.0 * np.pi * freq / (channels - 1)
    taper = 0.42323 - 0.49755 * np.cos(phase) + 0.07922 * np.cos(2.0 * phase)
    cos_part = np.cos(angle) * taper[None, :]
    sin_part = np.sin(angle) * taper[None, :]
    upper = np.stack([cos_part, sin_part], axis=-1)
    lower = np.stack([-sin_part, cos_part], axis=-1)
    return np.stack([upper, lower], axis=0).reshape(2 * channels, 2 * channels)


def in_hbm(x):
    return pltpu.with_memory_space_constraint(x, pltpu.HBM)


BATCH = 16
PUSH = 4


def chunks_of(groups):
    cuts = [32, 96, 128]
    if groups < 2 * sum(cuts):
        return [groups]
    return cuts + [groups - sum(cuts)]


def grid_kernel(
    live_hbm, tile_hbm, vis_hbm, weight_hbm, offset_hbm, grid_ref, wgrid_ref,
    live_ref, tile_ref, vis_ref, weight_ref, offset_ref, vis_sem, small_sem,
):
    rows, groups = vis_ref.shape[:2]
    cuts = chunks_of(groups)
    starts = [sum(cuts[:n]) for n in range(len(cuts))]

    def vis_copy(n):
        part = pl.ds(starts[n], cuts[n])
        return pltpu.make_async_copy(vis_hbm.at[:, part], vis_ref.at[:, part], vis_sem.at[n])

    head = sum(cuts[:2])
    pairs = [(live_hbm, live_ref), (tile_hbm, tile_ref)]
    later = []
    for source, target in ((offset_hbm, offset_ref), (weight_hbm, weight_ref)):
        pairs.append((source.at[pl.ds(0, head)], target.at[pl.ds(0, head)]))
        if head < groups:
            rest = pl.ds(head, groups - head)
            later.append((source.at[rest], target.at[rest]))
    small = [pltpu.make_async_copy(a, b, small_sem.at[n]) for n, (a, b) in enumerate(pairs)]
    later = [pltpu.make_async_copy(a, b, small_sem.at[len(pairs) + n]) for n, (a, b) in enumerate(later)]
    for copy in small:
        copy.start()
    for n in range(len(cuts)):
        vis_copy(n).start()
        if n == 1:
            for copy in later:
                copy.start()

    @pl.loop(0, grid_ref.shape[0] // 8)
    def _(i):
        some = pl.ds(i * 8, 8)
        grid_ref[some] = jnp.zeros((8, *grid_ref.shape[1:]), jnp.float32)
        wgrid_ref[some] = jnp.zeros((8, *wgrid_ref.shape[1:]), jnp.float32)

    for copy in small:
        copy.wait()

    cell = lax.broadcasted_iota(jnp.int32, (LANES, LANES), 0).astype(jnp.int16)
    lane = lax.broadcasted_iota(jnp.int32, (8, LANES), 1)
    sub = lax.broadcasted_iota(jnp.int32, (8, LANES), 0)
    zero = jnp.zeros((16, LANES), jnp.bfloat16)
    blank = jnp.zeros((HALVES * rows, LANES), jnp.bfloat16)

    def load(first):
        data = jnp.swapaxes(vis_ref[:, pl.ds(first, BATCH), :].astype(jnp.float32), 0, 1)
        return data, weight_ref[pl.ds(first, BATCH), :].astype(jnp.float32)

    def inner(*acc):
        sums, wsums = acc[:BATCH], acc[BATCH:]

        def feed(first, k, data, weights):
            hots, lefts, highs = [], [], []
            for i in range(PUSH):
                j = PUSH * k + i
                weight = jnp.where(lane < live_ref[0, first + j], jnp.broadcast_to(weights[j:j + 1], (8, LANES)), 0.0)
                offset = jnp.broadcast_to(offset_ref[pl.ds(first + j, 1), :], (8, LANES))
                low = jnp.bitwise_and(offset, LANES - 1)
                high = jnp.right_shift(offset, 7)
                low16 = jnp.concatenate([low, low], 0).astype(jnp.int16)
                weight16 = jnp.concatenate([weight, weight], 0).astype(jnp.bfloat16)
                hots.append(jnp.concatenate(
                    [jnp.where(cell[16 * q:16 * q + 16] == low16, weight16, zero) for q in range(LANES // 16)], 0
                ))
                highs.append(high)
                parts = [
                    jnp.where(high == a, data[j, 8 * q:8 * q + 8], 0.0) for a in range(HALVES) for q in range(rows // 8)
                ]
                left = jnp.concatenate(parts, 0).astype(jnp.bfloat16)
                lefts.append(jnp.concatenate([left, blank] if i % 2 == 0 else [blank, left], 1))
            ones = []
            for i in range(2):
                high = jnp.where(sub < 4, highs[i], highs[i + 2])
                mine = (jnp.bitwise_and(sub, 2) == 2 * i) & (high == jnp.bitwise_and(sub, 1))
                ones.append(jnp.where(mine, 1.0, 0.0))
            wleft = jnp.concatenate([jnp.concatenate(ones, 1), jnp.zeros((8, 2 * LANES), jnp.float32)], 0)
            turned = k >= BATCH // PUSH // 2
            if turned:
                hots = [hots[i].T for i in (0, 2, 1, 3)]
            right = jnp.concatenate([jnp.concatenate(hots[:2], 1), jnp.concatenate(hots[2:], 1)], 0)
            pltpu.matmul_push_rhs(right, k // 2, k % 2, transpose=not turned)
            for i in range(PUSH):
                pltpu.matmul_acc_lhs(sums[PUSH * k + i], lefts[i], load_staged_rhs=k // 2 if i == 0 else None)
            pltpu.matmul_acc_lhs(wsums[k], wleft.astype(jnp.bfloat16))

        def take(first, k):
            for i in range(PUSH):
                total = pltpu.matmul_pop(sums[PUSH * k + i])
                grid_ref[tile_ref[first + PUSH * k + i]] += total[:, :LANES] if i < 2 else total[:, LANES:]
            total = pltpu.matmul_pop(wsums[k])
            for i in range(PUSH):
                own = total[:8, :LANES] if i < 2 else total[:8, LANES:]
                wgrid_ref[tile_ref[first + PUSH * k + i]] += jnp.where(jnp.right_shift(sub, 1) == i, own, 0.0)

        def body(index, _):
            first = pl.multiple_of(index * BATCH, BATCH)
            data, weights = load(first)
            for k in range(BATCH // PUSH):
                take(first - BATCH, k)
                feed(first, k, data, weights)
            return 0

        vis_copy(0).wait()
        data, weights = load(0)
        for k in range(BATCH // PUSH):
            feed(0, k, data, weights)
        for n in range(len(cuts)):
            if n > 0:
                vis_copy(n).wait()
            if n == 2:
                for copy in later:
                    copy.wait()
            low, high = max(1, starts[n] // BATCH), (starts[n] + cuts[n]) // BATCH
            lax.fori_loop(low, high, body, 0, unroll=next((u for u in (16, 8, 4, 3, 2) if (high - low) % u == 0 and high - low > u), 1))
        for k in range(BATCH // PUSH):
            take(groups - BATCH, k)

    def space(unit, depth):
        return pltpu.ACC(unit)((depth, 2 * LANES), jnp.float32)

    pl.run_scoped(
        inner,
        *[space(k % 2, HALVES * rows) for k in range(BATCH // PUSH) for i in range(PUSH)],
        *[space(k % 2, 16) for k in range(BATCH // PUSH)],
    )


def gridding(data, weight, tiles, offset, live, n_tile):
    rows, groups, slots = data.shape
    hbm = pl.BlockSpec(memory_space=pltpu.HBM)
    vmem = pl.BlockSpec(memory_space=pltpu.VMEM)
    return pl.pallas_call(
        grid_kernel,
        in_specs=[hbm] * 5,
        out_specs=[vmem, vmem],
        out_shape=[
            jax.ShapeDtypeStruct((n_tile, HALVES * rows, LANES), jnp.float32),
            jax.ShapeDtypeStruct((n_tile, 8, LANES), jnp.float32),
        ],
        scratch_shapes=[
            pltpu.SMEM(live.shape, jnp.int32),
            pltpu.SMEM(tiles.shape, jnp.int32),
            pltpu.VMEM(data.shape, data.dtype),
            pltpu.VMEM(weight.shape, weight.dtype),
            pltpu.VMEM(offset.shape, jnp.int32),
            pltpu.SemaphoreType.DMA((len(chunks_of(groups)),)),
            pltpu.SemaphoreType.DMA((6,)),
        ],
        compiler_params=pltpu.CompilerParams(vmem_limit_bytes=24 << 20),
        cost_estimate=pl.CostEstimate(flops=2 * groups * rows * slots * TILE, bytes_accessed=data.size * 2, transcendentals=0),
        name="gridding",
    )(*[in_hbm(x) for x in (live, tiles, data, weight, offset)])


def dot3(left, right):
    dot = functools.partial(jnp.dot, preferred_element_type=jnp.float32)
    return dot(left[0], right[0]) + (dot(left[0], right[1]) + dot(left[1], right[0]))


def pair(x):
    high = x.astype(jnp.bfloat16)
    return high, (x - high.astype(jnp.float32)).astype(jnp.bfloat16)


def exchange_kernel(
    n_time, n_chan, per, grid_ref, wgrid_ref, delay_hbm, spread_hbm, out_ref,
    ring, mine, gathered, wown, wparts, delay, spread, scale,
    ring_send, ring_recv, plane_send, plane_recv, w_send, w_recv, table_sem,
):
    me_t = lax.axis_index("tm")
    me_c = lax.axis_index("chan")
    pieces = n_chan // per
    wide = pieces // 2
    reach = n_time // 2
    last = reach - 1
    fine = 2 if per % 2 == 0 else 1
    rows2 = grid_ref.shape[1]
    rows = rows2 // HALVES
    turn = me_c // per
    neighbour = (lax.rem(me_t + 1, n_time), lax.rem(me_t + n_time - 1, n_time))

    barrier = pltpu.get_barrier_semaphore()

    def greet_t(k, _):
        pl.semaphore_signal(barrier, inc=1, device_id={"tm": lax.rem(me_t + k, n_time)}, device_id_type=MESH)
        return 0

    def greet_c(k, _):
        pl.semaphore_signal(barrier, inc=1, device_id={"chan": lax.rem(me_c + k, n_chan)}, device_id_type=MESH)
        return 0

    greet_t(1, 0)
    greet_t(n_time - 1, 0)
    lax.fori_loop(2, n_time - 1, greet_t, 0)
    lax.fori_loop(1, n_chan, greet_c, 0)

    tables = [pltpu.make_async_copy(delay_hbm, delay, table_sem.at[0]),
              pltpu.make_async_copy(spread_hbm, spread, table_sem.at[1])]
    for copy in tables:
        copy.start()

    pl.semaphore_wait(barrier, n_time - 1 + n_chan - 1)

    def away(slot):
        if wide != 4:
            return lax.rem(slot + 1, wide)
        late = slot // 2
        return (2 + slot) * (1 - late) + (3 - slot) * late

    def pair_of(slot):
        return lax.rem(away(slot) + turn // 2, wide)

    def piece_of(slot):
        return 2 * pair_of(slot // 2) + lax.rem(slot + turn + 1, 2)

    def span(step, slot):
        if step < last:
            return pl.ds(pair_of(slot) * (2 * per), 2 * per)
        return pl.ds(piece_of(slot // fine) * per + lax.rem(slot, fine) * (per // fine), per // fine)

    def grid_span(chunk, step, slot):
        if step < last:
            return pl.ds(chunk * n_chan + pair_of(slot) * (2 * per), 2 * per)
        return pl.ds(chunk * n_chan + piece_of(slot // fine) * per + lax.rem(slot, fine) * (per // fine), per // fine)

    def chunk_of(way, step):
        hops = reach - step
        return lax.rem(me_t + (hops if way == 0 else n_time - hops), n_time)

    def ring_copy(way, step, slot, raw):
        where = span(step, slot)
        source = grid_ref.at[grid_span(chunk_of(way, step), step, slot)] if raw else ring.at[way, step - 1, where]
        return pltpu.make_async_remote_copy(
            src_ref=source,
            dst_ref=ring.at[way, step, where],
            send_sem=ring_send.at[way, step, slot],
            recv_sem=ring_recv.at[way, step, slot],
            device_id={"tm": neighbour[way]},
            device_id_type=MESH,
        )

    half = wide // 2

    def open_ring(slot, _):
        ring_copy(0, 0, slot, True).start()
        ring_copy(1, 0, slot + half, True).start()
        return 0

    lax.fori_loop(0, half, open_ring, 0)

    for t in range(n_time):
        part = wgrid_ref[t * n_chan + me_c]
        total = part[0:HALVES]
        for i in range(1, PUSH):
            total = total + part[HALVES * i:HALVES * (i + 1)]
        wown[t, 0:HALVES] = total

    def w_copy(k):
        other = lax.rem(me_t + k, n_time)
        return pltpu.make_async_remote_copy(
            src_ref=wown.at[other, pl.ds(0, HALVES)],
            dst_ref=wparts.at[k, pl.ds(0, HALVES)],
            send_sem=w_send.at[k],
            recv_sem=w_recv.at[k],
            device_id={"tm": other},
            device_id_type=MESH,
        )

    lax.fori_loop(1, n_time, lambda k, _: (w_copy(k).start(), 0)[1], 0)

    def hop(step, fresh):
        def body(slot, _):
            for way in range(2):
                if not fresh[way]:
                    ring_copy(way, step - 1, slot, True).wait_recv()
                    ring[way, step - 1, span(step - 1, slot)] += grid_ref[grid_span(chunk_of(way, step), step - 1, slot)]
                if step < last:
                    ring_copy(way, step, slot, fresh[way]).start()
            if step == last:
                for q in range(2 * fine):
                    for way in range(2):
                        ring_copy(way, step, 2 * fine * slot + q, fresh[way]).start()
            return 0
        return body

    lax.fori_loop(0, half, hop(1, (False, True)), 0)
    lax.fori_loop(half, wide, hop(1, (True, False)), 0)
    for step in range(2, reach):
        lax.fori_loop(0, wide, hop(step, (False, False)), 0)

    def plane_copy(other):
        return pltpu.make_async_remote_copy(
            src_ref=mine.at[other],
            dst_ref=gathered.at[me_c],
            send_sem=plane_send.at[other],
            recv_sem=plane_recv.at[me_c],
            device_id={"chan": other},
            device_id_type=MESH,
        )

    lax.fori_loop(1, n_time, lambda k, _: (w_copy(k).wait_recv(), 0)[1], 0)
    wsum = wown[me_t, 0:HALVES]
    for k in range(1, n_time):
        wsum = wsum + wparts[k, 0:HALVES]
    for copy in tables:
        copy.wait()
    wcells = jnp.concatenate([jnp.broadcast_to(wsum[a:a + 1], (8, LANES)) for a in range(HALVES)], 1)
    spread_pair = (spread[0], spread[1])
    scale[...] = jnp.broadcast_to(1.0 / jnp.maximum(dot3(pair(wcells), spread_pair), 1.0), scale.shape)

    def finish(slot, _):
        for way in range(2):
            ring_copy(way, last, slot, True).wait_recv()
        where = span(last, slot)
        mine[where] = grid_ref[grid_span(me_t, last, slot)] + ring[0, last, where] + ring[1, last, where]
        for q in range(per // fine):
            other = piece_of(slot // fine) * per + lax.rem(slot, fine) * (per // fine) + q

            @pl.when(other != me_c)
            def _():
                plane_copy(other).start()

            @pl.when(other == me_c)
            def _():
                gathered[me_c] = mine[me_c]
        return 0

    def absorb(slot, first):
        block = 2 * lax.rem(turn // 2 + wide - away(slot // 2), wide) + lax.rem(turn + pieces - slot - 1, 2)
        for q in range(per):
            other = block * per + q

            @pl.when(other != me_c)
            def _():
                pltpu.make_async_remote_copy(
                    src_ref=mine.at[other],
                    dst_ref=gathered.at[other],
                    send_sem=plane_send.at[other],
                    recv_sem=plane_recv.at[other],
                    device_id={"chan": other},
                    device_id_type=MESH,
                ).wait_recv()

        some = gathered[pl.ds(block * per, per)]
        cells = jnp.concatenate([some[:, a * rows:(a + 1) * rows, :].reshape(per * rows, LANES) for a in range(HALVES)], 1)
        normal = dot3(pair(cells), spread_pair) * scale[0:1]
        high, low = pair(normal)
        part = jnp.dot(delay[block], jnp.concatenate([high, high, low], 0), preferred_element_type=jnp.float32)
        out_ref[...] = part if first else out_ref[...] + part

    lag = min(3, pieces - 1)

    def whole(slot):
        for f in range(fine):
            finish(slot * fine + f, 0)

    def both(slot, _):
        absorb(slot - lag, False)
        whole(slot)
        return 0

    def drain_ring(way, step, low, high):
        lax.fori_loop(low, high, lambda slot, _: (ring_copy(way, step, slot, True).wait_send(), 0)[1], 0)

    drain_ring(0, 0, 0, half)
    drain_ring(1, 0, half, wide)
    for step in range(1, last):
        for way in range(2):
            drain_ring(way, step, 0, wide)
    lax.fori_loop(1, n_time, lambda k, _: (w_copy(k).wait_send(), 0)[1], 0)

    for slot in range(lag):
        whole(slot)
    absorb(0, True)
    whole(lag)
    lax.fori_loop(lag + 1, pieces, both, 0)
    for way in range(2):
        drain_ring(way, last, 0, pieces * fine)
    lax.fori_loop(pieces - lag, pieces - 1, lambda k, _: (absorb(k, False), 0)[1], 0)
    lax.fori_loop(1, n_chan, lambda k, _: (plane_copy(lax.rem(me_c + k, n_chan)).wait_send(), 0)[1], 0)
    absorb(pieces - 1, False)


def exchange(grid, wgrid, n_time, n_chan):
    rows2 = grid.shape[1]
    rows = rows2 // HALVES
    total = rows * n_chan
    per = max(1, n_chan // 8)
    pieces = n_chan // per
    reach = n_time // 2
    table = split_bf16(delay_table(total // 2)).reshape(2, total, pieces, per * rows)
    delay = jnp.asarray(np.concatenate([table[0], table[1], table[0]], -1).transpose(1, 0, 2))
    spread = jnp.asarray(split_bf16(spread_table()))
    vmem = pl.BlockSpec(memory_space=pltpu.VMEM)
    hbm = pl.BlockSpec(memory_space=pl.ANY)
    return pl.pallas_call(
        functools.partial(exchange_kernel, n_time, n_chan, per),
        in_specs=[vmem, vmem, hbm, hbm],
        out_specs=vmem,
        out_shape=jax.ShapeDtypeStruct((total, TILE), jnp.float32),
        scratch_shapes=[
            pltpu.VMEM((2, reach, n_chan, rows2, LANES), jnp.float32),
            pltpu.VMEM((n_chan, rows2, LANES), jnp.float32),
            pltpu.VMEM((n_chan, rows2, LANES), jnp.float32),
            pltpu.VMEM((n_time, 8, LANES), jnp.float32),
            pltpu.VMEM((n_time, 8, LANES), jnp.float32),
            pltpu.VMEM(delay.shape, jnp.bfloat16),
            pltpu.VMEM(spread.shape, jnp.bfloat16),
            pltpu.VMEM((8, TILE), jnp.float32),
            pltpu.SemaphoreType.DMA((2, reach, 2 * pieces)),
            pltpu.SemaphoreType.DMA((2, reach, 2 * pieces)),
            pltpu.SemaphoreType.DMA((n_chan,)),
            pltpu.SemaphoreType.DMA((n_chan,)),
            pltpu.SemaphoreType.DMA((n_time,)),
            pltpu.SemaphoreType.DMA((n_time,)),
            pltpu.SemaphoreType.DMA((2,)),
        ],
        compiler_params=pltpu.CompilerParams(collective_id=0, has_side_effects=True, vmem_limit_bytes=40 << 20),
        name="exchange",
    )(grid, wgrid, in_hbm(delay), in_hbm(spread))


def local(visibilities, vis_weight, tile_index, tile_offset, live_count):
    channels, parts, groups, slots = visibilities.shape
    n_chan = lax.axis_size("chan")
    n_time = lax.axis_size("tm")
    data = visibilities.reshape(channels * parts, groups, slots)
    grid, wgrid = gridding(data, vis_weight, tile_index, tile_offset, live_count, n_chan * n_time)
    result = exchange(grid, wgrid, n_time, n_chan)
    return result.reshape(2, channels * n_chan, TILE)


def solution(mesh):
    placed = (P("chan", None, "tm", None), P("tm", None), P("tm"), P("tm", None), P("tm", None))
    return jax.shard_map(
        local, mesh=mesh, in_specs=placed, out_specs=P(None, None, ("tm", "chan")), check_vma=False
    )
```
